128 devices in a mesh: gz: 2 (over x_hi), xy: 64 (over x_lo, y, z, core).
Axes of the slice: x: 4 (x_hi: 2, x_lo: 2; x = x_hi * 2 + x_lo), y: 4, z: 4, core: 2. Of those that a mesh axis runs over, the one named last changes fastest.
Arguments:
- section_image: bfloat16 [4, 256, 2048], P('gz', 'xy'), may hold values from -6 to 6
- crack_mask: int32 [4, 256, 2048], P('gz', 'xy'), may hold values 0 or 1
- fold_mask: int32 [4, 256, 2048], P('gz', 'xy'), may hold values 0 or 1
- first_weight: bfloat16 [9, 32], replicated, may hold values from -2 to 2
- first_bias: float32 [32], replicated, may hold values from -2 to 2
- second_weight: bfloat16 [9, 32, 32], replicated, may hold values from -0.5 to 0.5
- second_bias: float32 [32], replicated, may hold values from -2 to 2
- middle_weight: bfloat16 [27, 64, 32], replicated, may hold values from -0.3125 to 0.3125
- middle_bias: float32 [64], replicated, may hold values from -2 to 2
- deeper_weight: bfloat16 [27, 64, 64], replicated, may hold values from -0.21875 to 0.21875
- deeper_bias: float32 [64], replicated, may hold values from -2 to 2
- lift_weight: bfloat16 [32, 64], replicated, may hold values from -1 to 1
- lift_bias: float32 [32], replicated, may hold values from -2 to 2
- decode_weight: bfloat16 [9, 32, 32], replicated, may hold values from -0.5 to 0.5
- decode_bias: float32 [32], replicated, may hold values from -2 to 2
- head_weight: bfloat16 [3, 32], replicated, may hold values from -1.5 to 1.5
- head_bias: float32 [3], replicated, may hold values from -2 to 2
Outputs:
- affinity: float32 [3, 4, 2048, 256], P(None, 'gz', 'xy')
The draws below stay inside these ranges and needn't reach their ends.
All inputs are finite; a program needn't handle non-finite values. No bound on the sum of `crack_mask` or of `fold_mask` on one device may be relied on, other than what follows from the above.
Results may differ from the reference program's by a relative error of at most 0.0055.
Values may be sent and summed in bfloat16 or wider, within the bound.
A program may use at most 128 MiB of HBM per device.

```python
import math
import jax
import jax.numpy as jnp
from jax import lax

FINE_CH = 32
COARSE_CH = 64
COLS = 32
ROWS = 256
SECTIONS = 4
COLUMNS = 2048
N_XY = 64


def set_ends(result, stream_key, low, high):
    index_at = [jax.random.randint(jax.random.fold_in(stream_key, axis), (), 0, length) for axis, length in enumerate(result.shape)]
    main_axis = result.shape.index(max(result.shape))
    neighbour = index_at[:main_axis] + [(index_at[main_axis] + 1) % result.shape[main_axis]] + index_at[main_axis + 1:]
    return result.at[tuple(index_at)].set(low).at[tuple(neighbour)].set(high)


def level_of(rng, shape, split, least, largest):
    level = 1.0
    for position, blocks in split:
        steps = jax.random.uniform(jax.random.fold_in(jax.random.fold_in(rng, 6), position), (blocks,), jnp.float32, least / len(split), largest / len(split))
        level = level * jnp.repeat(jnp.exp(steps), shape[position] // blocks).reshape((-1,) + (1,) * (len(shape) - 1 - position))
    return level


def gaussian(rng, extent, scale, reach, split=(), kind=jnp.bfloat16):
    gain = level_of(rng, extent, split, -0.22, 0.18) if split else 1.0
    result = jax.random.normal(rng, extent, jnp.float32) * scale * gain
    return jnp.minimum(jnp.maximum(result, -reach), reach).astype(kind)


def setup_inputs(seed: int = 0) -> dict:
    arg_keys = jax.random.split(jax.random.key(seed), 18)
    section_image = gaussian(arg_keys[0], (SECTIONS, ROWS, COLUMNS), 1.0, 6.0, ((0, 2), (1, 64)))
    crack_mask = set_ends((jax.random.randint(arg_keys[1], (SECTIONS, ROWS, COLUMNS), 0, 16) < 1).astype(jnp.int32), jax.random.fold_in(arg_keys[1], 1), 0, 1)
    fold_mask = set_ends((jax.random.randint(arg_keys[2], (SECTIONS, ROWS, COLUMNS), 0, 16) < 1).astype(jnp.int32), jax.random.fold_in(arg_keys[2], 1), 0, 1)
    first_weight = gaussian(arg_keys[3], (9, FINE_CH), 9 ** -0.5, 2.0)
    first_bias = gaussian(arg_keys[4], (FINE_CH,), 0.5, 2.0, (), jnp.float32)
    second_weight = gaussian(arg_keys[5], (9, FINE_CH, FINE_CH), (9 * FINE_CH // 2) ** -0.5, 0.5)
    second_bias = gaussian(arg_keys[6], (FINE_CH,), 0.5, 2.0, (), jnp.float32)
    middle_weight = gaussian(arg_keys[7], (27, COARSE_CH, FINE_CH), (27 * FINE_CH // 2) ** -0.5, 0.3125)
    middle_bias = gaussian(arg_keys[8], (COARSE_CH,), 0.5, 2.0, (), jnp.float32)
    deeper_weight = gaussian(arg_keys[9], (27, COARSE_CH, COARSE_CH), (27 * COARSE_CH // 2) ** -0.5, 0.21875)
    deeper_bias = gaussian(arg_keys[10], (COARSE_CH,), 0.5, 2.0, (), jnp.float32)
    lift_weight = gaussian(arg_keys[11], (FINE_CH, COARSE_CH), (COARSE_CH // 2) ** -0.5, 1.0)
    lift_bias = gaussian(arg_keys[12], (FINE_CH,), 0.5, 2.0, (), jnp.float32)
    decode_weight = gaussian(arg_keys[13], (9, FINE_CH, FINE_CH), (9 * FINE_CH // 2) ** -0.5, 0.5)
    decode_bias = gaussian(arg_keys[14], (FINE_CH,), 0.5, 2.0, (), jnp.float32)
    head_weight = gaussian(arg_keys[15], (3, FINE_CH), (FINE_CH // 2) ** -0.5, 1.5)
    head_bias = gaussian(arg_keys[16], (3,), 0.5, 2.0, (), jnp.float32)
    return dict(section_image=section_image, crack_mask=crack_mask, fold_mask=fold_mask, first_weight=first_weight, first_bias=first_bias, second_weight=second_weight, second_bias=second_bias, middle_weight=middle_weight, middle_bias=middle_bias, deeper_weight=deeper_weight, deeper_bias=deeper_bias, lift_weight=lift_weight, lift_bias=lift_bias, decode_weight=decode_weight, decode_bias=decode_bias, head_weight=head_weight, head_bias=head_bias)


edge_margin = 16


def activate(summed, offset):
    return jax.nn.relu(summed + offset[:, None, None, None]).astype(jnp.bfloat16)


def stencil(padded, weight, depth_taps):
    out_z = padded.shape[1] - depth_taps + 1
    out_x = padded.shape[2] - 2
    out_y = padded.shape[3] - 2
    source = padded.astype(jnp.float32)
    kernel = weight.astype(jnp.float32)
    summed = jnp.zeros((weight.shape[1], out_z, out_x, out_y), jnp.float32)
    for shift_z in range(depth_taps):
        for shift_x in range(3):
            for shift_y in range(3):
                tap_slice = source[:, shift_z:shift_z + out_z, shift_x:shift_x + out_x, shift_y:shift_y + out_y]
                summed = summed + jnp.einsum("oc,czxy->ozxy", kernel[shift_z * 9 + shift_x * 3 + shift_y], tap_slice)
    return summed


def plane_pad(field):
    return jnp.pad(field, ((0, 0), (0, 0), (1, 1), (1, 1)))


def solid_pad(field):
    return jnp.pad(field, ((0, 0), (1, 1), (1, 1), (1, 1)))


def first_layer(slab_field, weight, offset):
    padded = jnp.pad(slab_field, ((0, 0), (1, 1), (1, 1))).astype(jnp.float32)
    out_x = slab_field.shape[1]
    out_y = slab_field.shape[2]
    summed = jnp.zeros((weight.shape[1],) + slab_field.shape, jnp.float32)
    for shift_x in range(3):
        for shift_y in range(3):
            tap_slice = padded[:, shift_x:shift_x + out_x, shift_y:shift_y + out_y]
            summed = summed + weight[shift_x * 3 + shift_y].astype(jnp.float32)[:, None, None, None] * tap_slice[None]
    return activate(summed, offset)


def reference(section_image, crack_mask, fold_mask, first_weight, first_bias, second_weight, second_bias, middle_weight, middle_bias, deeper_weight, deeper_bias, lift_weight, lift_bias, decode_weight, decode_bias, head_weight, head_bias):
    keep_mask = ((1 - crack_mask) * (1 - fold_mask)).astype(jnp.bfloat16)
    turned = jnp.transpose(section_image * keep_mask, (0, 2, 1))
    block_cols = COLS * math.gcd(N_XY, max(1, 512 // COLS))
    block_count = COLUMNS // block_cols
    span_cols = block_cols + 2 * edge_margin
    padded_volume = jnp.pad(turned, ((0, 0), (edge_margin, edge_margin), (0, 0)))
    zero_bf16 = jnp.zeros((), jnp.bfloat16)

    def one_block(block_start):
        slab_field = lax.dynamic_slice(padded_volume, (jnp.int32(0), block_start, jnp.int32(0)), (SECTIONS, span_cols, ROWS))
        fine_pos = block_start - edge_margin + lax.broadcasted_iota(jnp.int32, (1, 1, span_cols, 1), 2)
        fine_inside = (fine_pos >= 0) & (fine_pos < COLUMNS)
        coarse_pos = (block_start - edge_margin) // 2 + lax.broadcasted_iota(jnp.int32, (1, 1, span_cols // 2, 1), 2)
        coarse_inside = (coarse_pos >= 0) & (coarse_pos < COLUMNS // 2)
        encoded_one = jnp.where(fine_inside, first_layer(slab_field, first_weight, first_bias), zero_bf16)
        encoded_two = jnp.where(fine_inside, activate(stencil(plane_pad(encoded_one), second_weight, 1), second_bias), zero_bf16)
        channels = encoded_two.shape[0]
        pooled = encoded_two.reshape(channels, SECTIONS, span_cols // 2, 2, ROWS // 2, 2).max(axis=(3, 5))
        middle_one = jnp.where(coarse_inside, activate(stencil(solid_pad(pooled), middle_weight, 3), middle_bias), zero_bf16)
        middle_two = jnp.where(coarse_inside, activate(stencil(solid_pad(middle_one), deeper_weight, 3), deeper_bias), zero_bf16)
        lifted = jnp.einsum("oc,czxy->ozxy", lift_weight.astype(jnp.float32), middle_two.astype(jnp.float32)) + lift_bias[:, None, None, None]
        lifted_shape = lifted.shape
        spread = jnp.broadcast_to(lifted[:, :, :, None, :, None], (lifted_shape[0], lifted_shape[1], lifted_shape[2], 2, lifted_shape[3], 2))
        spread = spread.reshape(lifted_shape[0], lifted_shape[1], lifted_shape[2] * 2, lifted_shape[3] * 2)
        decoder_in = jnp.where(fine_inside, jax.nn.relu(spread + encoded_two.astype(jnp.float32)).astype(jnp.bfloat16), zero_bf16)
        decoded = activate(stencil(plane_pad(decoder_in), decode_weight, 1), decode_bias)
        logits = jnp.einsum("oc,czxy->ozxy", head_weight.astype(jnp.float32), decoded.astype(jnp.float32)) + head_bias[:, None, None, None]
        return jax.nn.sigmoid(logits)[:, :, edge_margin:edge_margin + block_cols, :]

    starts = jnp.arange(block_count, dtype=jnp.int32) * block_cols
    blocks = lax.map(one_block, starts)
    return jnp.transpose(blocks, (1, 2, 0, 3, 4)).reshape(3, SECTIONS, COLUMNS, ROWS)
```

```python
import jax
import jax.numpy as jnp
from jax import lax
from jax.experimental import pallas as pl
from jax.experimental.pallas import tpu as pltpu
from jax.sharding import PartitionSpec as P

BF16 = jnp.bfloat16
F32 = jnp.float32
MESH = pl.DeviceIdType.MESH
CHIPS = 32


def exchange_kernel(image_ref, crack_ref, fold_ref, strip_ref, band, tile, strip, a_send, a_recv, b_send, b_recv):
    gz = lax.axis_index("gz")
    xy = lax.axis_index("xy")
    core = lax.rem(xy, 2)
    chip = lax.div(xy, 2)
    twin = xy + 1 - 2 * core
    close = ((1 - gz, xy), (gz, twin), (1 - gz, twin))
    far = [(gz, 2 * lax.rem(chip + k, CHIPS) + core) for k in range(1, CHIPS)]

    barrier = pltpu.get_barrier_semaphore()
    for device in (*close, *far):
        pl.semaphore_signal(barrier, inc=1, device_id=device, device_id_type=MESH)

    keep = ((1 - crack_ref[...]) * (1 - fold_ref[...])).astype(F32)
    gated = image_ref[...].astype(F32) * keep
    gated = jnp.concatenate([gated[0], gated[1]], axis=0)
    band[0] = jnp.concatenate([gated[:, :1024], gated[:, 1024:]], axis=0).astype(BF16)

    pl.semaphore_wait(barrier, len(close) + len(far))
    copies = []
    for k, device in enumerate(close):
        copy = pltpu.make_async_remote_copy(
            src_ref=band.at[0], dst_ref=band.at[k + 1], send_sem=a_send.at[k], recv_sem=a_recv.at[k],
            device_id=device, device_id_type=MESH,
        )
        copy.start()
        copies.append(copy)
    for copy in copies:
        copy.wait()

    sub = lax.broadcasted_iota(jnp.int32, (8, 128), 0)
    lane = lax.broadcasted_iota(jnp.int32, (8, 128), 1)
    shift = jnp.where(core == 0, 16, 112)
    own = (lane >= 16 - 16 * core) & (lane < 128 - 16 * core)
    left = lane < 64
    windows = []
    for group in range(2):
        parts = []
        for c in range(2):
            slot = jnp.where(group == gz, 0, 1) + jnp.where(c == core, 0, 2)
            parts.append(band[slot].astype(F32))
        tiles = ([], [])
        for k in range(16):
            rows = slice(8 * (k // 8), 8 * (k // 8) + 8)
            lanes = slice(128 * (k % 8), 128 * (k % 8) + 128)
            low, high = parts[0][rows, lanes], parts[1][rows, lanes]
            zero = jnp.where(sub < 4, low, pltpu.roll(high, 4, 0))
            one = jnp.where(sub < 4, pltpu.roll(low, 4, 0), high)
            tiles[0].append(pltpu.roll(zero, shift, 1))
            tiles[1].append(pltpu.roll(one, shift, 1))
        found = []
        for q in range(2):
            moved = []
            for k in range(16):
                beside = jnp.where(core == 0, tiles[q][(k - 1) % 16], tiles[q][(k + 1) % 16])
                moved.append(jnp.where(own, tiles[q][k], beside))
            found.append(moved)
        windows.append(found)
    for k in range(16):
        even, odd = [], []
        for group in range(2):
            zero, one = windows[group][0][k], windows[group][1][k]
            even.append(jnp.where(left, zero, pltpu.roll(one, 64, 1)))
            odd.append(jnp.where(left, pltpu.roll(zero, 64, 1), one))
        tile[2 * k] = jnp.concatenate(even, axis=0).astype(BF16)
        tile[2 * k + 1] = jnp.concatenate(odd, axis=0).astype(BF16)

    for device in far:
        copy = pltpu.make_async_remote_copy(
            src_ref=tile.at[lax.div(device[1], 2)], dst_ref=strip.at[chip], send_sem=b_send, recv_sem=b_recv,
            device_id=device, device_id_type=MESH,
        )
        copy.start()
    strip[chip] = tile[chip]
    others = pl.ds(0, CHIPS - 1)
    pltpu.make_async_copy(strip.at[others], strip.at[others], b_recv).wait()
    strip_ref[...] = strip[...]
    pltpu.make_async_copy(tile.at[others], tile.at[others], b_send).wait()


def exchange(image, crack, fold, own_barrier=True):
    params = dict(collective_id=0) if own_barrier else {}
    return pl.pallas_call(
        exchange_kernel,
        out_shape=jax.ShapeDtypeStruct((CHIPS, 16, 128), BF16),
        in_specs=[pl.BlockSpec(memory_space=pltpu.VMEM)] * 3,
        out_specs=pl.BlockSpec(memory_space=pltpu.VMEM),
        scratch_shapes=[
            pltpu.VMEM((4, 16, 1024), BF16),
            pltpu.VMEM((CHIPS, 16, 128), BF16),
            pltpu.VMEM((CHIPS, 16, 128), BF16),
            pltpu.SemaphoreType.DMA((3,)),
            pltpu.SemaphoreType.DMA((3,)),
            pltpu.SemaphoreType.DMA,
            pltpu.SemaphoreType.DMA,
        ],
        compiler_params=pltpu.CompilerParams(has_side_effects=True, **params),
        name="exchange",
    )(image, crack, fold)


def iota(shape, dim):
    return lax.broadcasted_iota(jnp.int32, shape, dim)


def dot(lhs, rhs):
    return jnp.dot(lhs, rhs, preferred_element_type=F32)


def column_of(row):
    n = row.shape[1]
    eye = iota((n, n), 0) == iota((n, n), 1)
    return jnp.sum(jnp.where(eye, row, 0.0), axis=1, keepdims=True)


def neighbours(field):
    lanes = field.shape[1]
    lane = iota(field.shape, 1)
    below = jnp.where(lane == 0, 0.0, pltpu.roll(field, 1, 1))
    above = jnp.where(lane == lanes - 1, 0.0, pltpu.roll(field, lanes - 1, 1))
    return below, field, above


def relu_plus(summed, offset, channels):
    rows, lanes = summed.shape
    parts = summed.reshape(rows // channels, channels, lanes) + offset[None]
    return jnp.maximum(parts, 0.0).reshape(rows, lanes)


def band(weight_ref, band_ref, tap, blocks, group, span):
    out_ch, in_ch = weight_ref.shape[1], weight_ref.shape[2]
    band_ref[...] = jnp.zeros_like(band_ref)
    for block in range(blocks):
        for a in range(3):
            piece = weight_ref[tap(block, a)]
            for m in range(group):
                start = block * span + (m + a) * in_ch
                band_ref[m * out_ch : (m + 1) * out_ch, start : start + in_ch] = piece


def network_kernel(
    strip_ref,
    w1_ref, b1_ref, w2_ref, b2_ref, wm_ref, bm_ref, wd_ref, bd_ref, wl_ref, bl_ref, wc_ref, bc_ref, wh_ref, bh_ref,
    out_ref,
    t1, t2, tm, td, tc, tl, th,
    vol, one, two, joined, pooled, mid, deep, dec, last,
):
    gz = lax.axis_index("gz")
    xy = lax.axis_index("xy")
    first = xy == 0
    final = xy == lax.axis_size("xy") - 1

    base = jnp.zeros((32, 256), F32)
    lane = iota((32, 256), 1)
    w1 = w1_ref[...].astype(F32)
    for a in range(3):
        for b in range(3):
            col = column_of(w1[3 * a + b : 3 * a + b + 1])
            base = jnp.where(lane == 64 * b + a, col, base)

    @pl.loop(0, 46)
    def _(i):
        t1[pl.ds(pl.multiple_of(i * 32, 32), 32), :] = pltpu.roll(base, i, 1).astype(BF16)

    band(w2_ref, t2, lambda block, a: 3 * a + block, 3, 4, 192)
    band(wc_ref, tc, lambda block, a: 3 * a + block, 3, 4, 192)

    def solid_tap(block, a):
        e, b = divmod(block, 3)
        e = jnp.where(gz == 0, e, 2 - e)
        return 9 * e + 3 * a + b

    band(wm_ref, tm, solid_tap, 9, 4, 192)
    band(wd_ref, td, solid_tap, 9, 2, 256)
    tl[...] = jnp.zeros_like(tl)
    for m in range(4):
        tl[32 * m : 32 * m + 32, 64 * m : 64 * m + 64] = wl_ref[...]
    th[...] = jnp.zeros_like(th)
    wh = wh_ref[...].astype(F32)
    row = iota((24, 256), 0)
    lane = iota((24, 256), 1)
    spread_h = jnp.zeros((24, 256), F32)
    pick = (iota((32, 256), 0) == lax.rem(iota((32, 256), 1), 32)).astype(BF16)
    wide = dot(wh_ref[...], pick)
    for k in range(3):
        here = (row // 8 == k) & (row % 8 == lane // 32)
        spread_h = jnp.where(here, wide[k : k + 1], spread_h)
    th[...] = spread_h.astype(BF16)

    b1 = column_of(b1_ref[...])
    b2 = column_of(b2_ref[...])
    bm = column_of(bm_ref[...])
    bd = column_of(bd_ref[...])
    bl = column_of(bl_ref[...])
    bc = column_of(bc_ref[...])
    hrow = iota((24, 1), 0)
    bh_row = bh_ref[...]
    bh = jnp.where(hrow < 8, bh_row[:, 0:1], jnp.where(hrow < 16, bh_row[:, 1:2], bh_row[:, 2:3]))

    strip = strip_ref[...].astype(F32).reshape(32, 2, 8, 128)
    u = iota((64, 128), 0)
    l = iota((64, 128), 1)
    place = 32 * xy - 8 + u
    inside = (u < 48) & (place >= 0) & (place < 32 * lax.axis_size("xy"))
    for s in range(4):
        rows = strip[:, s // 2].reshape(256, 128).astype(BF16)
        select = jnp.where(inside & (l == 64 * (s % 2) + 8 + u), 1.0, 0.0).astype(BF16)
        turned = lax.dot_general(select, rows, (((1,), (1,)), ((), ())), preferred_element_type=F32)
        t = jnp.where(gz == 0, s, 3 - s)
        for b, part in enumerate(neighbours(turned)):
            vol[t, 64 * b : 64 * b + 64, :] = part.astype(BF16)

    @pl.loop(0, 4)
    def _(t):
        field = vol[t]
        for chunk in range(2):
            rows = slice(736 * chunk, 736 * chunk + 736)
            found = relu_plus(dot(t1[rows, 0:192], field), b1, 32)
            for b, part in enumerate(neighbours(found)):
                one[t, b, rows, :] = part.astype(BF16)

    @pl.when(first)
    def _():
        one[:, :, 0 : 7 * 32, :] = jnp.zeros((4, 3, 7 * 32, 256), BF16)

    @pl.when(final)
    def _():
        one[:, :, 39 * 32 : 46 * 32, :] = jnp.zeros((4, 3, 7 * 32, 256), BF16)

    @pl.loop(0, 11)
    def _(g):
        start = pl.multiple_of(g * 128, 128)
        half = pl.multiple_of(g * 64, 64)
        for t in range(4):
            field = jnp.concatenate([one[t, b, pl.ds(start, 192), :] for b in range(3)], axis=0)
            found = relu_plus(dot(t2[...], field), b2, 32)
            if t < 2:
                two[t, pl.ds(start, 128), :] = found.astype(BF16)
            pairs = found.reshape(2, 2, 32, 256)
            pairs = jnp.maximum(pairs[:, 0], pairs[:, 1]).reshape(64, 256)
            pairs = jnp.maximum(pairs, pltpu.roll(pairs, 255, 1))
            joined[t, pl.ds(half, 64), :] = pairs.astype(BF16)

    fine = iota((256, 384), 0)
    coarse = iota((256, 384), 1)
    pick = jnp.where(fine == 2 * (coarse % 128 + coarse // 128 - 1), 1.0, 0.0).astype(BF16)
    pooled[:, :, 0:128] = jnp.zeros((3, 704, 128), BF16)
    for t in range(4):
        found = dot(joined[t], pick).astype(BF16)
        for b in range(3):
            pooled[b, :, 128 * (t + 1) : 128 * (t + 2)] = found[:, 128 * b : 128 * b + 128]

    @pl.when(first)
    def _():
        pooled[:, 0:96, :] = jnp.zeros((3, 96, 640), BF16)

    @pl.when(final)
    def _():
        pooled[:, 19 * 32 : 22 * 32, :] = jnp.zeros((3, 96, 640), BF16)

    mid[:, :, 0:128] = jnp.zeros((3, 1280, 128), BF16)

    @pl.loop(0, 5)
    def _(g):
        start = pl.multiple_of(g * 128, 128)
        field = jnp.concatenate(
            [pooled[b, pl.ds(start, 192), 128 * e : 128 * e + 384] for e in range(3) for b in range(3)], axis=0
        )
        found = relu_plus(dot(tm[...], field), bm, 64)
        rows = pl.ds(pl.multiple_of(g * 256, 256), 256)
        for t in range(3):
            for b, part in enumerate(neighbours(found[:, 128 * t : 128 * t + 128])):
                mid[b, rows, 128 * (t + 1) : 128 * (t + 2)] = part.astype(BF16)

    @pl.when(first)
    def _():
        mid[:, 0:128, :] = jnp.zeros((3, 128, 512), BF16)

    @pl.when(final)
    def _():
        mid[:, 18 * 64 : 20 * 64, :] = jnp.zeros((3, 128, 512), BF16)

    @pl.loop(0, 9)
    def _(g):
        start = pl.multiple_of(g * 128, 128)
        field = jnp.concatenate(
            [mid[b, pl.ds(start, 256), 128 * e : 128 * e + 256] for e in range(3) for b in range(3)], axis=0
        )
        deep[pl.ds(start, 128), :] = relu_plus(dot(td[...], field), bd, 64).astype(BF16)

    fine = iota((256, 256), 1)
    coarse = iota((256, 256), 0)
    double = jnp.where(fine // 2 == coarse % 128, 1.0, 0.0).astype(BF16)
    for g in range(5):
        count = 4 if g < 4 else 2
        rows = dot(tl[0 : 32 * count, 0 : 64 * count], deep[256 * g : 256 * g + 64 * count, :])
        rows = (rows.reshape(count, 32, 256) + bl[None]).reshape(32 * count, 256)
        high = rows.astype(BF16)
        low = (rows - high.astype(F32)).astype(BF16)
        for t in range(2):
            both = jnp.concatenate([high[:, 128 * t : 128 * t + 128], low[:, 128 * t : 128 * t + 128]], axis=1)
            lifted = dot(both, double)
            for r in range(count):
                for p in range(2):
                    v = 2 * (4 * g + r) + p
                    old = two[t, 32 * (v + 4) : 32 * (v + 5), :].astype(F32)
                    found = jnp.maximum(lifted[32 * r : 32 * r + 32] + old, 0.0)
                    for b, part in enumerate(neighbours(found)):
                        dec[t, b, 32 * v : 32 * v + 32, :] = part.astype(BF16)

    @pl.when(first)
    def _():
        dec[:, :, 0:64, :] = jnp.zeros((2, 3, 64, 256), BF16)

    @pl.when(final)
    def _():
        dec[:, :, 34 * 32 : 36 * 32, :] = jnp.zeros((2, 3, 64, 256), BF16)

    @pl.loop(0, 4)
    def _(g):
        for t in range(2):
            parts = []
            for h in range(2):
                start = pl.multiple_of(g * 256 + 128 * h + 32, 32)
                field = jnp.concatenate([dec[t, b, pl.ds(start, 192), :] for b in range(3)], axis=0)
                parts.append(relu_plus(dot(tc[...], field), bc, 32).astype(BF16))
            logits = dot(th[...], jnp.concatenate(parts, axis=0)) + bh
            found = jax.nn.sigmoid(logits)
            s = jnp.where(gz == 0, t, 1 - t)
            for k in range(3):
                out_ref[k, s, pl.ds(pl.multiple_of(g * 8, 8), 8), :] = found[8 * k : 8 * k + 8]


def network(strip, *weights):
    scratch = [
        pltpu.VMEM((1472, 256), BF16),
        pltpu.VMEM((128, 576), BF16),
        pltpu.VMEM((256, 1728), BF16),
        pltpu.VMEM((128, 2304), BF16),
        pltpu.VMEM((128, 576), BF16),
        pltpu.VMEM((128, 256), BF16),
        pltpu.VMEM((24, 256), BF16),
        pltpu.VMEM((4, 192, 256), BF16),
        pltpu.VMEM((4, 3, 1472, 256), BF16),
        pltpu.VMEM((2, 1408, 256), BF16),
        pltpu.VMEM((4, 704, 256), BF16),
        pltpu.VMEM((3, 704, 640), BF16),
        pltpu.VMEM((3, 1280, 512), BF16),
        pltpu.VMEM((1152, 256), BF16),
        pltpu.VMEM((2, 3, 1152, 256), BF16),
        pltpu.VMEM((1024, 256), BF16),
    ]
    return pl.pallas_call(
        network_kernel,
        out_shape=jax.ShapeDtypeStruct((3, 2, 32, 256), F32),
        in_specs=[pl.BlockSpec(memory_space=pltpu.VMEM)] * 15,
        out_specs=pl.BlockSpec(memory_space=pltpu.VMEM),
        scratch_shapes=scratch,
        compiler_params=pltpu.CompilerParams(vmem_limit_bytes=48 * 1024 * 1024),
        name="network",
    )(strip, *weights)


def body(image, crack, fold, *weights):
    rows = [weight[None] if weight.ndim == 1 else weight for weight in weights]
    strip = exchange(image, crack, fold)
    return network(strip.reshape(CHIPS * 16, 128), *rows)


def solution(mesh):
    in_specs = (P("gz", "xy", None),) * 3 + (P(),) * 14
    out_specs = P(None, "gz", "xy", None)
    return jax.shard_map(body, mesh=mesh, in_specs=in_specs, out_specs=out_specs, check_vma=False)
```

```python
import jax
import jax.numpy as jnp
from jax import lax
from jax.experimental import pallas as pl
from jax.experimental.pallas import tpu as pltpu
from jax.sharding import PartitionSpec as P

BF16 = jnp.bfloat16
F32 = jnp.float32
MESH = pl.DeviceIdType.MESH
CHIPS = 32


def exchange_kernel(image_ref, crack_ref, fold_ref, strip_ref, band, tile, strip, a_send, a_recv, b_send, b_recv):
    gz = lax.axis_index("gz")
    xy = lax.axis_index("xy")
    core = lax.rem(xy, 2)
    chip = lax.div(xy, 2)
    twin = xy + 1 - 2 * core
    close = ((1 - gz, xy), (gz, twin), (1 - gz, twin))
    far = [(gz, 2 * lax.rem(chip + k, CHIPS) + core) for k in range(1, CHIPS)]

    barrier = pltpu.get_barrier_semaphore()
    for device in (*close, *far):
        pl.semaphore_signal(barrier, inc=1, device_id=device, device_id_type=MESH)

    keep = ((1 - crack_ref[...]) * (1 - fold_ref[...])).astype(F32)
    gated = image_ref[...].astype(F32) * keep
    gated = jnp.concatenate([gated[0], gated[1]], axis=0)
    band[0] = jnp.concatenate([gated[:, :1024], gated[:, 1024:]], axis=0).astype(BF16)

    pl.semaphore_wait(barrier, len(close) + len(far))
    copies = []
    for k, device in enumerate(close):
        copy = pltpu.make_async_remote_copy(
            src_ref=band.at[0], dst_ref=band.at[k + 1], send_sem=a_send.at[k], recv_sem=a_recv.at[k],
            device_id=device, device_id_type=MESH,
        )
        copy.start()
        copies.append(copy)
    for copy in copies:
        copy.wait()

    sub = lax.broadcasted_iota(jnp.int32, (8, 128), 0)
    lane = lax.broadcasted_iota(jnp.int32, (8, 128), 1)
    shift = jnp.where(core == 0, 16, 112)
    own = (lane >= 16 - 16 * core) & (lane < 128 - 16 * core)
    left = lane < 64
    windows = []
    for group in range(2):
        parts = []
        for c in range(2):
            slot = jnp.where(group == gz, 0, 1) + jnp.where(c == core, 0, 2)
            parts.append(band[slot].astype(F32))
        tiles = ([], [])
        for k in range(16):
            rows = slice(8 * (k // 8), 8 * (k // 8) + 8)
            lanes = slice(128 * (k % 8), 128 * (k % 8) + 128)
            low, high = parts[0][rows, lanes], parts[1][rows, lanes]
            zero = jnp.where(sub < 4, low, pltpu.roll(high, 4, 0))
            one = jnp.where(sub < 4, pltpu.roll(low, 4, 0), high)
            tiles[0].append(pltpu.roll(zero, shift, 1))
            tiles[1].append(pltpu.roll(one, shift, 1))
        found = []
        for q in range(2):
            moved = []
            for k in range(16):
                beside = jnp.where(core == 0, tiles[q][(k - 1) % 16], tiles[q][(k + 1) % 16])
                moved.append(jnp.where(own, tiles[q][k], beside))
            found.append(moved)
        windows.append(found)
    for k in range(16):
        even, odd = [], []
        for group in range(2):
            zero, one = windows[group][0][k], windows[group][1][k]
            even.append(jnp.where(left, zero, pltpu.roll(one, 64, 1)))
            odd.append(jnp.where(left, pltpu.roll(zero, 64, 1), one))
        tile[2 * k] = jnp.concatenate(even, axis=0).astype(BF16)
        tile[2 * k + 1] = jnp.concatenate(odd, axis=0).astype(BF16)

    for device in far:
        copy = pltpu.make_async_remote_copy(
            src_ref=tile.at[lax.div(device[1], 2)], dst_ref=strip.at[chip], send_sem=b_send, recv_sem=b_recv,
            device_id=device, device_id_type=MESH,
        )
        copy.start()
    strip[chip] = tile[chip]
    others = pl.ds(0, CHIPS - 1)
    pltpu.make_async_copy(strip.at[others], strip.at[others], b_recv).wait()
    strip_ref[...] = strip[...]
    pltpu.make_async_copy(tile.at[others], tile.at[others], b_send).wait()


def exchange(image, crack, fold, own_barrier=True):
    params = dict(collective_id=0) if own_barrier else {}
    return pl.pallas_call(
        exchange_kernel,
        out_shape=jax.ShapeDtypeStruct((CHIPS, 16, 128), BF16),
        in_specs=[pl.BlockSpec(memory_space=pltpu.VMEM)] * 3,
        out_specs=pl.BlockSpec(memory_space=pltpu.VMEM),
        scratch_shapes=[
            pltpu.VMEM((4, 16, 1024), BF16),
            pltpu.VMEM((CHIPS, 16, 128), BF16),
            pltpu.VMEM((CHIPS, 16, 128), BF16),
            pltpu.SemaphoreType.DMA((3,)),
            pltpu.SemaphoreType.DMA((3,)),
            pltpu.SemaphoreType.DMA,
            pltpu.SemaphoreType.DMA,
        ],
        compiler_params=pltpu.CompilerParams(has_side_effects=True, **params),
        name="exchange",
    )(image, crack, fold)


def iota(shape, dim):
    return lax.broadcasted_iota(jnp.int32, shape, dim)


def dot(lhs, rhs):
    return jnp.dot(lhs, rhs, preferred_element_type=F32)


def column_of(row):
    n = row.shape[1]
    eye = iota((n, n), 0) == iota((n, n), 1)
    return jnp.sum(jnp.where(eye, row, 0.0), axis=1, keepdims=True)


def neighbours(field):
    lanes = field.shape[1]
    lane = iota(field.shape, 1)
    below = jnp.where(lane == 0, 0.0, pltpu.roll(field, 1, 1))
    above = jnp.where(lane == lanes - 1, 0.0, pltpu.roll(field, lanes - 1, 1))
    return below, field, above


def relu_plus(summed, offset, channels):
    rows, lanes = summed.shape
    parts = summed.reshape(rows // channels, channels, lanes) + offset[None]
    return jnp.maximum(parts, 0.0).reshape(rows, lanes)


def band(weight_ref, band_ref, tap, blocks, group, span):
    out_ch, in_ch = weight_ref.shape[1], weight_ref.shape[2]
    band_ref[...] = jnp.zeros_like(band_ref)
    for block in range(blocks):
        for a in range(3):
            piece = weight_ref[tap(block, a)]
            for m in range(group):
                start = block * span + (m + a) * in_ch
                band_ref[m * out_ch : (m + 1) * out_ch, start : start + in_ch] = piece


def network_kernel(
    strip_ref,
    w1_ref, b1_ref, w2_ref, b2_ref, wm_ref, bm_ref, wd_ref, bd_ref, wl_ref, bl_ref, wc_ref, bc_ref, wh_ref, bh_ref,
    out_ref,
    t1, t2, tm, td, tc, tl, th,
    vol, one, two, joined, pooled, mid, deep, dec, last,
):
    gz = lax.axis_index("gz")
    xy = lax.axis_index("xy")
    first = xy == 0
    final = xy == lax.axis_size("xy") - 1

    base = jnp.zeros((32, 256), F32)
    lane = iota((32, 256), 1)
    w1 = w1_ref[...].astype(F32)
    for a in range(3):
        for b in range(3):
            col = column_of(w1[3 * a + b : 3 * a + b + 1])
            base = jnp.where(lane == 64 * b + a, col, base)

    @pl.loop(0, 46)
    def _(i):
        t1[pl.ds(pl.multiple_of(i * 32, 32), 32), :] = pltpu.roll(base, i, 1).astype(BF16)

    band(w2_ref, t2, lambda block, a: 3 * a + block, 3, 4, 192)
    band(wc_ref, tc, lambda block, a: 3 * a + block, 3, 4, 192)

    def solid_tap(block, a):
        e, b = divmod(block, 3)
        e = jnp.where(gz == 0, e, 2 - e)
        return 9 * e + 3 * a + b

    band(wm_ref, tm, solid_tap, 9, 4, 192)
    band(wd_ref, td, solid_tap, 9, 2, 256)
    tl[...] = jnp.zeros_like(tl)
    for m in range(4):
        tl[32 * m : 32 * m + 32, 64 * m : 64 * m + 64] = wl_ref[...]
    th[...] = jnp.zeros_like(th)
    wh = wh_ref[...].astype(F32)
    row = iota((24, 256), 0)
    lane = iota((24, 256), 1)
    spread_h = jnp.zeros((24, 256), F32)
    pick = (iota((32, 256), 0) == lax.rem(iota((32, 256), 1), 32)).astype(BF16)
    wide = dot(wh_ref[...], pick)
    for k in range(3):
        here = (row // 8 == k) & (row % 8 == lane // 32)
        spread_h = jnp.where(here, wide[k : k + 1], spread_h)
    th[...] = spread_h.astype(BF16)

    b1 = column_of(b1_ref[...])
    b2 = column_of(b2_ref[...])
    bm = column_of(bm_ref[...])
    bd = column_of(bd_ref[...])
    bl = column_of(bl_ref[...])
    bc = column_of(bc_ref[...])
    hrow = iota((24, 1), 0)
    bh_row = bh_ref[...]
    bh = jnp.where(hrow < 8, bh_row[:, 0:1], jnp.where(hrow < 16, bh_row[:, 1:2], bh_row[:, 2:3]))

    strip = strip_ref[...].astype(F32).reshape(32, 2, 8, 128)
    u = iota((64, 128), 0)
    l = iota((64, 128), 1)
    place = 32 * xy - 8 + u
    inside = (u < 48) & (place >= 0) & (place < 32 * lax.axis_size("xy"))
    for s in range(4):
        rows = strip[:, s // 2].reshape(256, 128).astype(BF16)
        select = jnp.where(inside & (l == 64 * (s % 2) + 8 + u), 1.0, 0.0).astype(BF16)
        turned = lax.dot_general(select, rows, (((1,), (1,)), ((), ())), preferred_element_type=F32)
        t = jnp.where(gz == 0, s, 3 - s)
        for b, part in enumerate(neighbours(turned)):
            vol[t, 64 * b : 64 * b + 64, :] = part.astype(BF16)

    @pl.loop(0, 4, unroll=4)
    def _(t):
        field = vol[t]
        for chunk in range(2):
            rows = slice(736 * chunk, 736 * chunk + 736)
            found = relu_plus(dot(t1[rows, 0:192], field), b1, 32)
            for b, part in enumerate(neighbours(found)):
                one[t, b, rows, :] = part.astype(BF16)

    @pl.when(first)
    def _():
        one[:, :, 0 : 7 * 32, :] = jnp.zeros((4, 3, 7 * 32, 256), BF16)

    @pl.when(final)
    def _():
        one[:, :, 39 * 32 : 46 * 32, :] = jnp.zeros((4, 3, 7 * 32, 256), BF16)

    @pl.loop(0, 11, unroll=11)
    def _(g):
        start = pl.multiple_of(g * 128, 128)
        half = pl.multiple_of(g * 64, 64)
        for t in range(4):
            field = jnp.concatenate([one[t, b, pl.ds(start, 192), :] for b in range(3)], axis=0)
            found = relu_plus(dot(t2[...], field), b2, 32)
            if t < 2:
                two[t, pl.ds(start, 128), :] = found.astype(BF16)
            pairs = found.reshape(2, 2, 32, 256)
            pairs = jnp.maximum(pairs[:, 0], pairs[:, 1]).reshape(64, 256)
            pairs = jnp.maximum(pairs, pltpu.roll(pairs, 255, 1))
            joined[t, pl.ds(half, 64), :] = pairs.astype(BF16)

    fine = iota((256, 384), 0)
    coarse = iota((256, 384), 1)
    pick = jnp.where(fine == 2 * (coarse % 128 + coarse // 128 - 1), 1.0, 0.0).astype(BF16)
    pooled[:, :, 0:128] = jnp.zeros((3, 704, 128), BF16)
    for t in range(4):
        found = dot(joined[t], pick).astype(BF16)
        for b in range(3):
            pooled[b, :, 128 * (t + 1) : 128 * (t + 2)] = found[:, 128 * b : 128 * b + 128]

    @pl.when(first)
    def _():
        pooled[:, 0:96, :] = jnp.zeros((3, 96, 640), BF16)

    @pl.when(final)
    def _():
        pooled[:, 19 * 32 : 22 * 32, :] = jnp.zeros((3, 96, 640), BF16)

    mid[:, :, 0:128] = jnp.zeros((3, 1280, 128), BF16)

    @pl.loop(0, 5, unroll=5)
    def _(g):
        start = pl.multiple_of(g * 128, 128)
        field = jnp.concatenate(
            [pooled[b, pl.ds(start, 192), 128 * e : 128 * e + 384] for e in range(3) for b in range(3)], axis=0
        )
        found = relu_plus(dot(tm[...], field), bm, 64)
        rows = pl.ds(pl.multiple_of(g * 256, 256), 256)
        for t in range(3):
            for b, part in enumerate(neighbours(found[:, 128 * t : 128 * t + 128])):
                mid[b, rows, 128 * (t + 1) : 128 * (t + 2)] = part.astype(BF16)

    @pl.when(first)
    def _():
        mid[:, 0:128, :] = jnp.zeros((3, 128, 512), BF16)

    @pl.when(final)
    def _():
        mid[:, 18 * 64 : 20 * 64, :] = jnp.zeros((3, 128, 512), BF16)

    @pl.loop(0, 9, unroll=9)
    def _(g):
        start = pl.multiple_of(g * 128, 128)
        field = jnp.concatenate(
            [mid[b, pl.ds(start, 256), 128 * e : 128 * e + 256] for e in range(3) for b in range(3)], axis=0
        )
        deep[pl.ds(start, 128), :] = relu_plus(dot(td[...], field), bd, 64).astype(BF16)

    fine = iota((256, 256), 1)
    coarse = iota((256, 256), 0)
    double = jnp.where(fine // 2 == coarse % 128, 1.0, 0.0).astype(BF16)
    for g in range(5):
        count = 4 if g < 4 else 2
        rows = dot(tl[0 : 32 * count, 0 : 64 * count], deep[256 * g : 256 * g + 64 * count, :])
        rows = (rows.reshape(count, 32, 256) + bl[None]).reshape(32 * count, 256)
        high = rows.astype(BF16)
        low = (rows - high.astype(F32)).astype(BF16)
        for t in range(2):
            both = jnp.concatenate([high[:, 128 * t : 128 * t + 128], low[:, 128 * t : 128 * t + 128]], axis=1)
            lifted = dot(both, double)
            for r in range(count):
                for p in range(2):
                    v = 2 * (4 * g + r) + p
                    old = two[t, 32 * (v + 4) : 32 * (v + 5), :].astype(F32)
                    found = jnp.maximum(lifted[32 * r : 32 * r + 32] + old, 0.0)
                    for b, part in enumerate(neighbours(found)):
                        dec[t, b, 32 * v : 32 * v + 32, :] = part.astype(BF16)

    @pl.when(first)
    def _():
        dec[:, :, 0:64, :] = jnp.zeros((2, 3, 64, 256), BF16)

    @pl.when(final)
    def _():
        dec[:, :, 34 * 32 : 36 * 32, :] = jnp.zeros((2, 3, 64, 256), BF16)

    @pl.loop(0, 4, unroll=4)
    def _(g):
        for t in range(2):
            parts = []
            for h in range(2):
                start = pl.multiple_of(g * 256 + 128 * h + 32, 32)
                field = jnp.concatenate([dec[t, b, pl.ds(start, 192), :] for b in range(3)], axis=0)
                parts.append(relu_plus(dot(tc[...], field), bc, 32).astype(BF16))
            logits = dot(th[...], jnp.concatenate(parts, axis=0)) + bh
            found = jax.nn.sigmoid(logits)
            s = jnp.where(gz == 0, t, 1 - t)
            for k in range(3):
                out_ref[k, s, pl.ds(pl.multiple_of(g * 8, 8), 8), :] = found[8 * k : 8 * k + 8]


def network(strip, *weights):
    scratch = [
        pltpu.VMEM((1472, 256), BF16),
        pltpu.VMEM((128, 576), BF16),
        pltpu.VMEM((256, 1728), BF16),
        pltpu.VMEM((128, 2304), BF16),
        pltpu.VMEM((128, 576), BF16),
        pltpu.VMEM((128, 256), BF16),
        pltpu.VMEM((24, 256), BF16),
        pltpu.VMEM((4, 192, 256), BF16),
        pltpu.VMEM((4, 3, 1472, 256), BF16),
        pltpu.VMEM((2, 1408, 256), BF16),
        pltpu.VMEM((4, 704, 256), BF16),
        pltpu.VMEM((3, 704, 640), BF16),
        pltpu.VMEM((3, 1280, 512), BF16),
        pltpu.VMEM((1152, 256), BF16),
        pltpu.VMEM((2, 3, 1152, 256), BF16),
        pltpu.VMEM((1024, 256), BF16),
    ]
    return pl.pallas_call(
        network_kernel,
        out_shape=jax.ShapeDtypeStruct((3, 2, 32, 256), F32),
        in_specs=[pl.BlockSpec(memory_space=pltpu.VMEM)] * 15,
        out_specs=pl.BlockSpec(memory_space=pltpu.VMEM),
        scratch_shapes=scratch,
        compiler_params=pltpu.CompilerParams(vmem_limit_bytes=48 * 1024 * 1024),
        name="network",
    )(strip, *weights)


def body(image, crack, fold, *weights):
    rows = [weight[None] if weight.ndim == 1 else weight for weight in weights]
    strip = exchange(image, crack, fold)
    return network(strip.reshape(CHIPS * 16, 128), *rows)


def solution(mesh):
    in_specs = (P("gz", "xy", None),) * 3 + (P(),) * 14
    out_specs = P(None, "gz", "xy", None)
    return jax.shard_map(body, mesh=mesh, in_specs=in_specs, out_specs=out_specs, check_vma=False)
```

```python
import jax
import jax.numpy as jnp
from jax import lax
from jax.experimental import pallas as pl
from jax.experimental.pallas import tpu as pltpu
from jax.sharding import PartitionSpec as P

BF16 = jnp.bfloat16
F32 = jnp.float32
MESH = pl.DeviceIdType.MESH
CHIPS = 32


def iota(shape, dim):
    return lax.broadcasted_iota(jnp.int32, shape, dim)


def dot(lhs, rhs):
    return jnp.dot(lhs, rhs, preferred_element_type=F32)


def dot_turned(lhs, rhs):
    return lax.dot_general(lhs, rhs, (((1,), (1,)), ((), ())), preferred_element_type=F32)


def column_of(row):
    n = row.shape[1]
    eye = iota((n, n), 0) == iota((n, n), 1)
    return jnp.sum(jnp.where(eye, row, 0.0), axis=1, keepdims=True)


def neighbours(field):
    lanes = field.shape[1]
    lane = iota(field.shape, 1)
    below = jnp.where(lane == 0, 0.0, pltpu.roll(field, 1, 1))
    above = jnp.where(lane == lanes - 1, 0.0, pltpu.roll(field, lanes - 1, 1))
    return below, field, above


def relu_plus(summed, offset, channels, low=0, high=0, keep_low=None, keep_high=None):
    rows, lanes = summed.shape
    count = rows // channels
    parts = jnp.maximum(summed.reshape(count, channels, lanes) + offset[None], 0.0)
    if low or high:
        pieces = []
        if low:
            pieces.append(parts[:low] * keep_low)
        pieces.append(parts[low : count - high])
        if high:
            pieces.append(parts[count - high :] * keep_high)
        parts = jnp.concatenate([piece for piece in pieces if piece.shape[0]], axis=0)
    return parts.reshape(rows, lanes)


def widen(piece):
    rows, lanes = piece.shape
    return jnp.concatenate([piece.astype(F32), jnp.zeros((rows, 128 - lanes), F32)], axis=1)


def plane_band(weight_ref, band_ref):
    lane = iota((32, 128), 1)
    tiles = [[None] * 5 for _ in range(4)]
    for b in range(3):
        pieces = [widen(weight_ref[3 * a + b]) for a in range(3)]
        base = pieces[0] + pltpu.roll(pieces[1], 32, 1) + pltpu.roll(pieces[2], 64, 1)
        for m in range(4):
            start = 192 * b + 32 * m
            at, off = start // 128, start % 128
            moved = pltpu.roll(base, off, 1) if off else base
            shares = [(at, moved)]
            if off + 96 > 128:
                shares = [(at, jnp.where(lane >= off, moved, 0.0)), (at + 1, jnp.where(lane < off - 32, moved, 0.0))]
            for tile, share in shares:
                old = tiles[m][tile]
                tiles[m][tile] = share if old is None else old + share
    zero = jnp.zeros((32, 128), F32)
    for m in range(4):
        row = [zero if tile is None else tile for tile in tiles[m]]
        band_ref[32 * m : 32 * m + 32, :] = jnp.concatenate(row, axis=1)[:, 0:576].astype(BF16)


def kernel(
    image_hbm, crack_hbm, fold_hbm,
    w1_hbm, b1_hbm, w2_hbm, b2_hbm, wm_hbm, bm_hbm, wd_hbm, bd_hbm, wl_hbm, bl_hbm, wc_hbm, bc_hbm, wh_hbm, bh_hbm,
    out_ref,
    image_ref, crack_ref, fold_ref,
    w1_ref, b1_ref, w2_ref, b2_ref, wm_ref, bm_ref, wd_ref, bd_ref, wl_ref, bl_ref, wc_ref, bc_ref, wh_ref, bh_ref,
    load_sem, swap_send, swap_recv, far_send, far_recv, pass_send, pass_recv,
    half, tile, strip,
    t1, t2, tm, td, tc, tl, th, stack,
    vol, one, two, joined, pooled, mid, deep, dec,
):
    gz = lax.axis_index("gz")
    xy = lax.axis_index("xy")
    core = lax.rem(xy, 2)
    chip = lax.div(xy, 2)
    last_xy = lax.axis_size("xy") - 1
    keep_low = jnp.where(xy == 0, 0.0, 1.0)
    keep_high = jnp.where(xy == last_xy, 0.0, 1.0)
    twin = (gz, xy + 1 - 2 * core)

    sources = (
        image_hbm, crack_hbm, fold_hbm,
        w1_hbm, b1_hbm, w2_hbm, b2_hbm, wm_hbm, bm_hbm, wd_hbm, bd_hbm, wl_hbm, bl_hbm, wc_hbm, bc_hbm, wh_hbm, bh_hbm,
    )
    targets = (
        image_ref, crack_ref, fold_ref,
        w1_ref, b1_ref, w2_ref, b2_ref, wm_ref, bm_ref, wd_ref, bd_ref, wl_ref, bl_ref, wc_ref, bc_ref, wh_ref, bh_ref,
    )
    loads = [pltpu.make_async_copy(s, t, load_sem.at[i]) for i, (s, t) in enumerate(zip(sources, targets))]
    for load in loads:
        load.start()

    barrier = pltpu.get_barrier_semaphore()
    pl.semaphore_signal(barrier, inc=1, device_id=twin, device_id_type=MESH)
    source_gz = jnp.where(core == 1, gz, 1 - gz)
    target_gz = jnp.where(core == 0, gz, 1 - gz)

    @pl.loop(0, CHIPS, unroll=True)
    def _(k):
        other = lax.rem(chip + k, CHIPS)
        pl.semaphore_signal(barrier, inc=1, device_id=(source_gz, 2 * other + 1 - core), device_id_type=MESH)

    for load in loads[:3]:
        load.wait()
    keep = ((1 - crack_ref[...]) * (1 - fold_ref[...])).astype(F32)
    gated = image_ref[...].astype(F32) * keep
    gated = jnp.concatenate([gated[0], gated[1]], axis=0)
    half[core] = jnp.concatenate([gated[:, :1024], gated[:, 1024:]], axis=0).astype(BF16)

    pl.semaphore_wait(barrier, CHIPS + 1)
    swap = pltpu.make_async_remote_copy(
        src_ref=half.at[core], dst_ref=half.at[core], send_sem=swap_send, recv_sem=swap_recv,
        device_id=twin, device_id_type=MESH,
    )
    swap.start()
    swap.wait()

    sub = iota((8, 128), 0)
    lane = iota((8, 128), 1)
    bands = (half[0].astype(F32), half[1].astype(F32))
    moved = []
    for q in range(2):
        evens, odds = [], []
        for k in range(16):
            rows = slice(8 * (k // 8), 8 * (k // 8) + 8)
            lanes = slice(128 * (k % 8), 128 * (k % 8) + 128)
            low, high = bands[0][rows, lanes], bands[1][rows, lanes]
            if q == 0:
                both = jnp.where(sub < 4, low, pltpu.roll(high, 4, 0))
            else:
                both = jnp.where(sub < 4, pltpu.roll(low, 4, 0), high)
            evens.append(pltpu.roll(both, 16, 1))
            odds.append(pltpu.roll(both, 80, 1))
        moved.append((evens, odds))
    for k in range(16):
        even = [jnp.where(lane >= 16, moved[q][0][k], moved[q][0][max(k - 1, 0)]) for q in range(2)]
        odd = [jnp.where(lane < 80, moved[q][1][k], moved[q][1][min(k + 1, 15)]) for q in range(2)]
        tile[2 * k] = jnp.concatenate(even, axis=0).astype(BF16)
        tile[2 * k + 1] = jnp.concatenate(odd, axis=0).astype(BF16)

    @pl.loop(0, CHIPS, unroll=True)
    def _(k):
        other = lax.rem(chip + k, CHIPS)
        pltpu.make_async_remote_copy(
            src_ref=tile.at[other], dst_ref=strip.at[0, chip], send_sem=far_send, recv_sem=far_recv,
            device_id=(target_gz, 2 * other + 1 - core), device_id_type=MESH,
        ).start()

    for load in loads[3:]:
        load.wait()
    base = [jnp.zeros((32, 128), F32), jnp.zeros((32, 128), F32)]
    lane = iota((32, 128), 1)
    w1 = w1_ref[...].astype(F32)
    for a in range(3):
        for b in range(3):
            col = column_of(w1[3 * a + b : 3 * a + b + 1])
            base[b // 2] = jnp.where(lane == 64 * (b % 2) + a, col, base[b // 2])
    for i in range(46):
        for n in range(2):
            t1[32 * i : 32 * i + 32, 128 * n : 128 * n + 128] = pltpu.roll(base[n], i, 1).astype(BF16)

    plane_band(w2_ref, t2)
    plane_band(wc_ref, tc)

    eye = (iota((64, 64), 0) == iota((64, 64), 1)).astype(BF16)
    stack[...] = jnp.zeros_like(stack)
    for e in range(3):
        place = jnp.where(gz == 0, e, 2 - e)
        for b in range(3):
            block = 3 * e + b
            for m in range(4):
                for a in range(3):
                    start = 192 * block + 32 * (m + a)
                    stack[m, start : start + 32, :] = wm_ref[9 * place + 3 * a + b]
            pieces = [widen(wd_ref[9 * place + 3 * a + b]) for a in range(3)]
            turned = [pltpu.roll(piece, 64, 1) for piece in pieces]
            rows = ((pieces[0] + turned[1], pieces[2]), (turned[0], pieces[1] + turned[2]))
            for m in range(2):
                for n in range(2):
                    start = 256 * block + 128 * n
                    td[64 * m : 64 * m + 64, start : start + 128] = rows[m][n].astype(BF16)
    for m in range(4):
        tm[64 * m : 64 * m + 64, :] = dot_turned(eye, stack[m]).astype(BF16)

    lift = widen(wl_ref[...])
    turned = pltpu.roll(lift, 64, 1)
    blank = jnp.zeros((32, 128), F32)
    for m in range(4):
        piece = turned if m % 2 else lift
        row = [piece, blank] if m < 2 else [blank, piece]
        tl[32 * m : 32 * m + 32, :] = jnp.concatenate(row, axis=1).astype(BF16)
    pick = (iota((32, 256), 0) == lax.rem(iota((32, 256), 1), 32)).astype(BF16)
    wide = dot(wh_ref[...], pick)
    row = iota((24, 256), 0)
    lane = iota((24, 256), 1)
    heads = jnp.zeros((24, 256), F32)
    for k in range(3):
        here = (row // 8 == k) & (row % 8 == lane // 32)
        heads = jnp.where(here, wide[k : k + 1], heads)
    th[...] = heads.astype(BF16)

    b1 = column_of(b1_ref[...])
    b2 = column_of(b2_ref[...])
    bm = column_of(bm_ref[...])
    bd = column_of(bd_ref[...])
    bl = column_of(bl_ref[...])
    bc = column_of(bc_ref[...])
    hrow = iota((24, 1), 0)
    bh_row = bh_ref[...]
    bh = jnp.where(hrow < 8, bh_row[:, 0:1], jnp.where(hrow < 16, bh_row[:, 1:2], bh_row[:, 2:3]))

    pltpu.make_async_copy(strip.at[0], strip.at[0], far_recv).wait()
    hand = pltpu.make_async_remote_copy(
        src_ref=strip.at[0], dst_ref=strip.at[1], send_sem=pass_send, recv_sem=pass_recv,
        device_id=twin, device_id_type=MESH,
    )
    hand.start()

    u = iota((64, 128), 0)
    l = iota((64, 128), 1)
    place = 32 * xy - 8 + u
    inside = (u < 48) & (place >= 0) & (place < 32 * (last_xy + 1))
    select = jnp.where(inside & (l == 8 + 32 * core + u), 1.0, 0.0).astype(BF16)

    for source in range(2):
        if source == 1:
            hand.wait()
        first_t = 2 * (1 - core) if source == 0 else 2 * core
        tiles = strip[source].astype(F32).reshape(CHIPS, 2, 8, 128)
        for q in range(2):
            t = first_t + jnp.where(gz == 0, q, 1 - q)
            rows = tiles[:, q].reshape(256, 128).astype(BF16)
            turned = dot_turned(select, rows)
            for b, part in enumerate(neighbours(turned)):
                vol[t, 64 * b : 64 * b + 64, :] = part.astype(BF16)
            field = vol[t]
            for chunk in range(2):
                rows = slice(736 * chunk, 736 * chunk + 736)
                found = dot(t1[rows, 0:192], field)
                if chunk == 0:
                    found = relu_plus(found, b1, 32, low=7, keep_low=keep_low)
                else:
                    found = relu_plus(found, b1, 32, high=7, keep_high=keep_high)
                for b, part in enumerate(neighbours(found)):
                    one[t, b, rows, :] = part.astype(BF16)

        @pl.loop(0, 11, unroll=True)
        def _(g):
            start = pl.multiple_of(g * 128, 128)
            halved = pl.multiple_of(g * 64, 64)
            for q in range(2):
                t = first_t + q
                field = jnp.concatenate([one[t, b, pl.ds(start, 192), :] for b in range(3)], axis=0)
                found = relu_plus(dot(t2[...], field), b2, 32)
                two[t, pl.ds(start, 128), :] = found.astype(BF16)
                pairs = found.reshape(2, 2, 32, 256)
                pairs = jnp.maximum(pairs[:, 0], pairs[:, 1]).reshape(64, 256)
                pairs = jnp.maximum(pairs, pltpu.roll(pairs, 255, 1))
                joined[t, pl.ds(halved, 64), :] = pairs.astype(BF16)

    fine = iota((256, 384), 0)
    coarse = iota((256, 384), 1)
    pick = jnp.where(fine == 2 * (coarse % 128 + coarse // 128 - 1), 1.0, 0.0).astype(BF16)
    pooled[:, :, 0:128] = jnp.zeros((3, 704, 128), BF16)
    for t in range(4):
        found = dot(joined[t], pick)
        found = jnp.concatenate([found[:96] * keep_low, found[96:608], found[608:] * keep_high], axis=0).astype(BF16)
        for b in range(3):
            pooled[b, :, 128 * (t + 1) : 128 * (t + 2)] = found[:, 128 * b : 128 * b + 128]

    mid[:, :, 0:128] = jnp.zeros((3, 1280, 128), BF16)
    for g in range(5):
        field = jnp.concatenate(
            [pooled[b, 128 * g : 128 * g + 192, 128 * e : 128 * e + 384] for e in range(3) for b in range(3)], axis=0
        )
        found = dot(tm[...], field)
        low, high = (2, 0) if g == 0 else (0, 2) if g == 4 else (0, 0)
        found = relu_plus(found, bm, 64, low, high, keep_low, keep_high)
        for t in range(3):
            for b, part in enumerate(neighbours(found[:, 128 * t : 128 * t + 128])):
                mid[b, 256 * g : 256 * g + 256, 128 * (t + 1) : 128 * (t + 2)] = part.astype(BF16)

    @pl.loop(0, 9, unroll=True)
    def _(g):
        start = pl.multiple_of(g * 128, 128)
        field = jnp.concatenate(
            [mid[b, pl.ds(start, 256), 128 * e : 128 * e + 256] for e in range(3) for b in range(3)], axis=0
        )
        deep[pl.ds(start, 128), :] = relu_plus(dot(td[...], field), bd, 64).astype(BF16)

    fine = iota((256, 256), 1)
    coarse = iota((256, 256), 0)
    double = jnp.where(fine // 2 == coarse % 128, 1.0, 0.0).astype(BF16)
    for g in range(5):
        count = 4 if g < 4 else 2
        rows = dot(tl[0 : 32 * count, 0 : 64 * count], deep[256 * g : 256 * g + 64 * count, :])
        rows = (rows.reshape(count, 32, 256) + bl[None]).reshape(32 * count, 256)
        high = rows.astype(BF16)
        low = (rows - high.astype(F32)).astype(BF16)
        for t in range(2):
            both = jnp.concatenate([high[:, 128 * t : 128 * t + 128], low[:, 128 * t : 128 * t + 128]], axis=1)
            lifted = dot(both, double)
            for r in range(count):
                for p in range(2):
                    v = 2 * (4 * g + r) + p
                    old = two[t, 32 * (v + 4) : 32 * (v + 5), :].astype(F32)
                    found = jnp.maximum(lifted[32 * r : 32 * r + 32] + old, 0.0)
                    if v < 2:
                        found = found * keep_low
                    if v >= 34:
                        found = found * keep_high
                    for b, part in enumerate(neighbours(found)):
                        dec[t, b, 32 * v : 32 * v + 32, :] = part.astype(BF16)

    @pl.loop(0, 4, unroll=True)
    def _(g):
        for t in range(2):
            parts = []
            for h in range(2):
                start = pl.multiple_of(g * 256 + 128 * h + 32, 32)
                field = jnp.concatenate([dec[t, b, pl.ds(start, 192), :] for b in range(3)], axis=0)
                parts.append(relu_plus(dot(tc[...], field), bc, 32).astype(BF16))
            logits = dot(th[...], jnp.concatenate(parts, axis=0)) + bh
            found = jax.nn.sigmoid(logits)
            s = jnp.where(gz == 0, t, 1 - t)
            for k in range(3):
                out_ref[k, s, pl.ds(pl.multiple_of(g * 8, 8), 8), :] = found[8 * k : 8 * k + 8]

    pltpu.make_async_copy(tile, tile, far_send).wait()


def body(image, crack, fold, *weights):
    rows = [weight[None] if weight.ndim == 1 else weight for weight in weights]
    rows[4] = jnp.swapaxes(rows[4], 1, 2)
    operands = (image, crack, fold, *rows)
    dma = pltpu.SemaphoreType.DMA
    scratch = [pltpu.VMEM(operand.shape, operand.dtype) for operand in operands]
    scratch += [dma((len(operands),)), dma, dma, dma, dma, dma, dma]
    scratch += [
        pltpu.VMEM(shape, BF16)
        for shape in (
            (2, 16, 1024), (CHIPS, 16, 128), (2, CHIPS, 16, 128),
            (1472, 256), (128, 576), (256, 1728), (128, 2304), (128, 576), (128, 256), (24, 256), (4, 1728, 64),
            (4, 192, 256), (4, 3, 1472, 256), (4, 1408, 256), (4, 704, 256), (3, 704, 640), (3, 1280, 512),
            (1152, 256), (2, 3, 1152, 256),
        )
    ]
    return pl.pallas_call(
        kernel,
        out_shape=jax.ShapeDtypeStruct((3, 2, 32, 256), F32),
        in_specs=[pl.BlockSpec(memory_space=pl.ANY)] * len(operands),
        out_specs=pl.BlockSpec(memory_space=pltpu.VMEM),
        scratch_shapes=scratch,
        compiler_params=pltpu.CompilerParams(
            collective_id=0, has_side_effects=True, vmem_limit_bytes=60 * 1024 * 1024
        ),
        name="window",
    )(*operands)


def solution(mesh):
    in_specs = (P("gz", "xy", None),) * 3 + (P(),) * 14
    out_specs = P(None, "gz", "xy", None)
    return jax.shard_map(body, mesh=mesh, in_specs=in_specs, out_specs=out_specs, check_vma=False)
```

```python
import jax
import jax.numpy as jnp
from jax import lax
from jax.experimental import pallas as pl
from jax.experimental.pallas import tpu as pltpu
from jax.sharding import PartitionSpec as P

BF16 = jnp.bfloat16
F32 = jnp.float32
MESH = pl.DeviceIdType.MESH
CHIPS = 32


def iota(shape, dim):
    return lax.broadcasted_iota(jnp.int32, shape, dim)


def dot(lhs, rhs):
    return jnp.dot(lhs, rhs, preferred_element_type=F32)


def dot_turned(lhs, rhs):
    return lax.dot_general(lhs, rhs, (((1,), (1,)), ((), ())), preferred_element_type=F32)


def column_of(row):
    n = row.shape[1]
    eye = iota((n, n), 0) == iota((n, n), 1)
    return jnp.sum(jnp.where(eye, row, 0.0), axis=1, keepdims=True)


def neighbours(field):
    lanes = field.shape[1]
    lane = iota(field.shape, 1)
    below = jnp.where(lane == 0, 0.0, pltpu.roll(field, 1, 1))
    above = jnp.where(lane == lanes - 1, 0.0, pltpu.roll(field, lanes - 1, 1))
    return below, field, above


def relu_plus(summed, offset, channels, low=0, high=0, keep_low=None, keep_high=None):
    rows, lanes = summed.shape
    count = rows // channels
    parts = jnp.maximum(summed.reshape(count, channels, lanes) + offset[None], 0.0)
    if low or high:
        pieces = []
        if low:
            pieces.append(parts[:low] * keep_low)
        pieces.append(parts[low : count - high])
        if high:
            pieces.append(parts[count - high :] * keep_high)
        parts = jnp.concatenate([piece for piece in pieces if piece.shape[0]], axis=0)
    return parts.reshape(rows, lanes)


def gather_rows(summed, channels):
    rows, lanes = summed.shape
    taps = summed.reshape(rows // (3 * channels), 3, channels, lanes)
    below, here, above = (taps[:, b].reshape(rows // 3, lanes) for b in range(3))
    lane = iota((rows // 3, 128), 1)
    parts = []
    for n in range(lanes // 128):
        block = slice(128 * n, 128 * n + 128)
        parts.append(
            here[:, block]
            + jnp.where(lane == 0, 0.0, pltpu.roll(below[:, block], 1, 1))
            + jnp.where(lane == 127, 0.0, pltpu.roll(above[:, block], 127, 1))
        )
    return jnp.concatenate(parts, axis=1)


def widen(piece):
    rows, lanes = piece.shape
    return jnp.concatenate([piece.astype(F32), jnp.zeros((rows, 128 - lanes), F32)], axis=1)


def plane_band(weight_ref, band_ref):
    lane = iota((32, 128), 1)
    tiles = [[None] * 5 for _ in range(4)]
    for b in range(3):
        pieces = [widen(weight_ref[3 * a + b]) for a in range(3)]
        base = pieces[0] + pltpu.roll(pieces[1], 32, 1) + pltpu.roll(pieces[2], 64, 1)
        for m in range(4):
            start = 192 * b + 32 * m
            at, off = start // 128, start % 128
            moved = pltpu.roll(base, off, 1) if off else base
            shares = [(at, moved)]
            if off + 96 > 128:
                shares = [(at, jnp.where(lane >= off, moved, 0.0)), (at + 1, jnp.where(lane < off - 32, moved, 0.0))]
            for tile, share in shares:
                old = tiles[m][tile]
                tiles[m][tile] = share if old is None else old + share
    zero = jnp.zeros((32, 128), F32)
    for m in range(4):
        row = [zero if tile is None else tile for tile in tiles[m]]
        band_ref[32 * m : 32 * m + 32, :] = jnp.concatenate(row, axis=1)[:, 0:576].astype(BF16)


def kernel(
    image_hbm, crack_hbm, fold_hbm,
    w1_hbm, b1_hbm, w2_hbm, b2_hbm, wm_hbm, bm_hbm, wd_hbm, bd_hbm, wl_hbm, bl_hbm, wc_hbm, bc_hbm, wh_hbm, bh_hbm,
    out_ref,
    image_ref, crack_ref, fold_ref,
    w1_ref, b1_ref, w2_ref, b2_ref, wm_ref, bm_ref, wd_ref, bd_ref, wl_ref, bl_ref, wc_ref, bc_ref, wh_ref, bh_ref,
    load_sem, swap_send, swap_recv, far_send, far_recv, pass_send, pass_recv,
    half, tile, strip,
    t1, t2, tm, td, tc, tl, th,
    vol, one, two, joined, pooled, mid, deep, dec,
):
    gz = lax.axis_index("gz")
    xy = lax.axis_index("xy")
    core = lax.rem(xy, 2)
    chip = lax.div(xy, 2)
    last_xy = lax.axis_size("xy") - 1
    keep_low = jnp.where(xy == 0, 0.0, 1.0)
    keep_high = jnp.where(xy == last_xy, 0.0, 1.0)
    twin = (gz, xy + 1 - 2 * core)

    x, y, z = lax.div(chip, 16), lax.rem(lax.div(chip, 4), 4), lax.rem(chip, 4)
    steps = [(i, j, k) for i in range(2) for j in range(4) for k in range(4)]
    steps.sort(key=lambda step: -(2 - abs(2 - step[1]) + 2 - abs(2 - step[2])))
    others = [16 * lax.rem(x + i, 2) + 4 * lax.rem(y + j, 4) + lax.rem(z + k, 4) for i, j, k in steps]

    sources = (
        image_hbm, crack_hbm, fold_hbm,
        w1_hbm, b1_hbm, w2_hbm, b2_hbm, wm_hbm, bm_hbm, wd_hbm, bd_hbm, wl_hbm, bl_hbm, wc_hbm, bc_hbm, wh_hbm, bh_hbm,
    )
    targets = (
        image_ref, crack_ref, fold_ref,
        w1_ref, b1_ref, w2_ref, b2_ref, wm_ref, bm_ref, wd_ref, bd_ref, wl_ref, bl_ref, wc_ref, bc_ref, wh_ref, bh_ref,
    )
    loads = [pltpu.make_async_copy(s, t, load_sem.at[i]) for i, (s, t) in enumerate(zip(sources, targets))]
    for load in loads:
        load.start()

    barrier = pltpu.get_barrier_semaphore()
    pl.semaphore_signal(barrier, inc=1, device_id=twin, device_id_type=MESH)
    source_gz = jnp.where(core == 1, gz, 1 - gz)
    target_gz = jnp.where(core == 0, gz, 1 - gz)

    for other in others:
        pl.semaphore_signal(barrier, inc=1, device_id=(source_gz, 2 * other + 1 - core), device_id_type=MESH)

    for load in loads[:3]:
        load.wait()
    keep = ((1 - crack_ref[...]) * (1 - fold_ref[...])).astype(F32)
    gated = image_ref[...].astype(F32) * keep
    gated = jnp.concatenate([gated[0], gated[1]], axis=0)
    half[core] = jnp.concatenate([gated[:, :1024], gated[:, 1024:]], axis=0).astype(BF16)

    pl.semaphore_wait(barrier, CHIPS + 1)
    swap = pltpu.make_async_remote_copy(
        src_ref=half.at[core], dst_ref=half.at[core], send_sem=swap_send, recv_sem=swap_recv,
        device_id=twin, device_id_type=MESH,
    )
    swap.start()
    swap.wait()

    sub = iota((8, 128), 0)
    lane = iota((8, 128), 1)
    bands = (half[0].astype(F32), half[1].astype(F32))
    moved = []
    for q in range(2):
        evens, odds = [], []
        for k in range(16):
            rows = slice(8 * (k // 8), 8 * (k // 8) + 8)
            lanes = slice(128 * (k % 8), 128 * (k % 8) + 128)
            low, high = bands[0][rows, lanes], bands[1][rows, lanes]
            if q == 0:
                both = jnp.where(sub < 4, low, pltpu.roll(high, 4, 0))
            else:
                both = jnp.where(sub < 4, pltpu.roll(low, 4, 0), high)
            evens.append(pltpu.roll(both, 16, 1))
            odds.append(pltpu.roll(both, 80, 1))
        moved.append((evens, odds))
    for k in range(16):
        even = [jnp.where(lane >= 16, moved[q][0][k], moved[q][0][max(k - 1, 0)]) for q in range(2)]
        odd = [jnp.where(lane < 80, moved[q][1][k], moved[q][1][min(k + 1, 15)]) for q in range(2)]
        tile[2 * k] = jnp.concatenate(even, axis=0).astype(BF16)
        tile[2 * k + 1] = jnp.concatenate(odd, axis=0).astype(BF16)

    for other in others:
        pltpu.make_async_remote_copy(
            src_ref=tile.at[other], dst_ref=strip.at[0, chip], send_sem=far_send, recv_sem=far_recv,
            device_id=(target_gz, 2 * other + 1 - core), device_id_type=MESH,
        ).start()

    for load in loads[3:]:
        load.wait()
    base = [jnp.zeros((32, 128), F32), jnp.zeros((32, 128), F32)]
    lane = iota((32, 128), 1)
    w1 = w1_ref[...].astype(F32)
    for a in range(3):
        for b in range(3):
            col = column_of(w1[3 * a + b : 3 * a + b + 1])
            base[b // 2] = jnp.where(lane == 64 * (b % 2) + a, col, base[b // 2])
    for i in range(46):
        for n in range(2):
            t1[32 * i : 32 * i + 32, 128 * n : 128 * n + 128] = pltpu.roll(base[n], i, 1).astype(BF16)

    plane_band(w2_ref, t2)
    plane_band(wc_ref, tc)

    eye = (iota((64, 64), 0) == iota((64, 64), 1)).astype(BF16)
    for e in range(3):
        place = jnp.where(gz == 0, e, 2 - e)
        for b in range(3):
            rows = [wm_ref[9 * place + 3 * a + b] for a in range(3)]
            base = dot_turned(eye, jnp.concatenate([*rows, jnp.zeros((32, 64), BF16)], axis=0))
            for m in range(2):
                moved = pltpu.roll(base, 32, 1) if m else base
                start = 192 * m + 64 * b
                tm[start : start + 64, 128 * e : 128 * e + 128] = moved.astype(BF16)
            pieces = [widen(wd_ref[9 * place + 3 * a + b]) for a in range(3)]
            turned = [pltpu.roll(piece, 64, 1) for piece in pieces]
            rows = ((pieces[0] + turned[1], pieces[2]), (turned[0], pieces[1] + turned[2]))
            for m in range(2):
                start = 192 * m + 64 * b
                for n in range(2):
                    td[start : start + 64, 256 * e + 128 * n : 256 * e + 128 * n + 128] = rows[m][n].astype(BF16)

    lift = widen(wl_ref[...])
    turned = pltpu.roll(lift, 64, 1)
    blank = jnp.zeros((32, 128), F32)
    for m in range(4):
        piece = turned if m % 2 else lift
        row = [piece, blank] if m < 2 else [blank, piece]
        tl[32 * m : 32 * m + 32, :] = jnp.concatenate(row, axis=1).astype(BF16)
    pick = (iota((32, 256), 0) == lax.rem(iota((32, 256), 1), 32)).astype(BF16)
    wide = dot(wh_ref[...], pick)
    row = iota((24, 256), 0)
    lane = iota((24, 256), 1)
    heads = jnp.zeros((24, 256), F32)
    for k in range(3):
        here = (row // 8 == k) & (row % 8 == lane // 32)
        heads = jnp.where(here, wide[k : k + 1], heads)
    th[...] = heads.astype(BF16)

    b1 = column_of(b1_ref[...])
    b2 = column_of(b2_ref[...])
    bm = column_of(bm_ref[...])
    bd = column_of(bd_ref[...])
    bl = column_of(bl_ref[...])
    bc = column_of(bc_ref[...])
    hrow = iota((24, 1), 0)
    bh_row = bh_ref[...]
    bh = jnp.where(hrow < 8, bh_row[:, 0:1], jnp.where(hrow < 16, bh_row[:, 1:2], bh_row[:, 2:3]))

    pltpu.make_async_copy(strip.at[0], strip.at[0], far_recv).wait()
    hand = pltpu.make_async_remote_copy(
        src_ref=strip.at[0], dst_ref=strip.at[1], send_sem=pass_send, recv_sem=pass_recv,
        device_id=twin, device_id_type=MESH,
    )
    hand.start()

    u = iota((64, 128), 0)
    l = iota((64, 128), 1)
    place = 32 * xy - 8 + u
    inside = (u < 48) & (place >= 0) & (place < 32 * (last_xy + 1))
    select = jnp.where(inside & (l == 8 + 32 * core + u), 1.0, 0.0).astype(BF16)

    for source in range(2):
        if source == 1:
            hand.wait()
        first_t = 2 * (1 - core) if source == 0 else 2 * core
        tiles = strip[source].astype(F32).reshape(CHIPS, 2, 8, 128)
        for q in range(2):
            t = first_t + jnp.where(gz == 0, q, 1 - q)
            rows = tiles[:, q].reshape(256, 128).astype(BF16)
            turned = dot_turned(select, rows)
            for b, part in enumerate(neighbours(turned)):
                vol[t, 64 * b : 64 * b + 64, :] = part.astype(BF16)
            field = vol[t]
            for chunk in range(2):
                rows = slice(736 * chunk, 736 * chunk + 736)
                found = dot(t1[rows, 0:192], field)
                if chunk == 0:
                    found = relu_plus(found, b1, 32, low=7, keep_low=keep_low)
                else:
                    found = relu_plus(found, b1, 32, high=7, keep_high=keep_high)
                for b, part in enumerate(neighbours(found)):
                    one[t, b, rows, :] = part.astype(BF16)

        @pl.loop(0, 11, unroll=True)
        def _(g):
            start = pl.multiple_of(g * 128, 128)
            halved = pl.multiple_of(g * 64, 64)
            for q in range(2):
                t = first_t + q
                field = jnp.concatenate([one[t, b, pl.ds(start, 192), :] for b in range(3)], axis=0)
                found = relu_plus(dot(t2[...], field), b2, 32)
                two[t, pl.ds(start, 128), :] = found.astype(BF16)
                pairs = found.reshape(2, 2, 32, 256)
                pairs = jnp.maximum(pairs[:, 0], pairs[:, 1]).reshape(64, 256)
                pairs = jnp.maximum(pairs, pltpu.roll(pairs, 255, 1))
                joined[t, pl.ds(halved, 64), :] = pairs.astype(BF16)

    fine = iota((256, 128), 0)
    coarse = iota((256, 128), 1)
    pick = jnp.where(fine == 2 * coarse, 1.0, 0.0).astype(BF16)
    pooled[:, 0:128] = jnp.zeros((704, 128), BF16)
    for t in range(4):
        found = dot(joined[t], pick)
        found = jnp.concatenate([found[:96] * keep_low, found[96:608], found[608:] * keep_high], axis=0).astype(BF16)
        pooled[:, 128 * (t + 1) : 128 * (t + 2)] = found

    mid[:, 0:128] = jnp.zeros((1280, 128), BF16)
    for g in range(5):
        field = []
        for e in range(3):
            near = [pooled[128 * g + 64 * h : 128 * g + 64 * h + 128, 128 * e : 128 * e + 384] for h in range(2)]
            field.append(jnp.concatenate([near[0][:, :256], near[1][:, :256], near[0][:, 256:], near[1][:, 256:]], axis=1))
        found = gather_rows(dot(tm[...], jnp.concatenate(field, axis=0)), 64)
        found = jnp.maximum(found.reshape(2, 64, 768) + bm[None], 0.0).reshape(128, 768)
        for h in range(2):
            part = jnp.concatenate([found[:, 256 * h : 256 * h + 256], found[:, 512 + 128 * h : 640 + 128 * h]], axis=1)
            if g == 0 and h == 0:
                part = part * keep_low
            if g == 4 and h == 1:
                part = part * keep_high
            mid[256 * g + 128 * h : 256 * g + 128 * h + 128, 128:512] = part.astype(BF16)

    for g in range(9):
        field = jnp.concatenate([mid[128 * g : 128 * g + 256, 128 * e : 128 * e + 256] for e in range(3)], axis=0)
        found = gather_rows(dot(td[...], field), 64)
        deep[128 * g : 128 * g + 128, :] = jnp.maximum(found.reshape(2, 64, 256) + bd[None], 0.0).reshape(128, 256).astype(BF16)

    fine = iota((256, 256), 1)
    coarse = iota((256, 256), 0)
    double = jnp.where(fine // 2 == coarse % 128, 1.0, 0.0).astype(BF16)
    for g in range(5):
        count = 4 if g < 4 else 2
        rows = dot(tl[0 : 32 * count, 0 : 64 * count], deep[256 * g : 256 * g + 64 * count, :])
        rows = (rows.reshape(count, 32, 256) + bl[None]).reshape(32 * count, 256)
        high = rows.astype(BF16)
        low = (rows - high.astype(F32)).astype(BF16)
        for t in range(2):
            both = jnp.concatenate([high[:, 128 * t : 128 * t + 128], low[:, 128 * t : 128 * t + 128]], axis=1)
            lifted = dot(both, double)
            for r in range(count):
                for p in range(2):
                    v = 2 * (4 * g + r) + p
                    old = two[t, 32 * (v + 4) : 32 * (v + 5), :].astype(F32)
                    found = jnp.maximum(lifted[32 * r : 32 * r + 32] + old, 0.0)
                    if v < 2:
                        found = found * keep_low
                    if v >= 34:
                        found = found * keep_high
                    for b, part in enumerate(neighbours(found)):
                        dec[t, b, 32 * v : 32 * v + 32, :] = part.astype(BF16)

    @pl.loop(0, 4, unroll=True)
    def _(g):
        for t in range(2):
            parts = []
            for h in range(2):
                start = pl.multiple_of(g * 256 + 128 * h + 32, 32)
                field = jnp.concatenate([dec[t, b, pl.ds(start, 192), :] for b in range(3)], axis=0)
                parts.append(relu_plus(dot(tc[...], field), bc, 32).astype(BF16))
            logits = dot(th[...], jnp.concatenate(parts, axis=0)) + bh
            found = jax.nn.sigmoid(logits)
            s = jnp.where(gz == 0, t, 1 - t)
            for k in range(3):
                out_ref[k, s, pl.ds(pl.multiple_of(g * 8, 8), 8), :] = found[8 * k : 8 * k + 8]

    pltpu.make_async_copy(tile, tile, far_send).wait()


def body(image, crack, fold, *weights):
    rows = [weight[None] if weight.ndim == 1 else weight for weight in weights]
    rows[4] = jnp.swapaxes(rows[4], 1, 2)
    operands = (image, crack, fold, *rows)
    dma = pltpu.SemaphoreType.DMA
    scratch = [pltpu.VMEM(operand.shape, operand.dtype) for operand in operands]
    scratch += [dma((len(operands),)), dma, dma, dma, dma, dma, dma]
    scratch += [
        pltpu.VMEM(shape, BF16)
        for shape in (
            (2, 16, 1024), (CHIPS, 16, 128), (2, CHIPS, 16, 128),
            (1472, 256), (128, 576), (384, 384), (384, 768), (128, 576), (128, 256), (24, 256),
            (4, 192, 256), (4, 3, 1472, 256), (4, 1408, 256), (4, 704, 256), (704, 640), (1280, 512),
            (1152, 256), (2, 3, 1152, 256),
        )
    ]
    return pl.pallas_call(
        kernel,
        out_shape=jax.ShapeDtypeStruct((3, 2, 32, 256), F32),
        in_specs=[pl.BlockSpec(memory_space=pl.ANY)] * len(operands),
        out_specs=pl.BlockSpec(memory_space=pltpu.VMEM),
        scratch_shapes=scratch,
        compiler_params=pltpu.CompilerParams(
            collective_id=0, has_side_effects=True, vmem_limit_bytes=60 * 1024 * 1024
        ),
        name="window",
    )(*operands)


def solution(mesh):
    in_specs = (P("gz", "xy", None),) * 3 + (P(),) * 14
    out_specs = P(None, "gz", "xy", None)
    return jax.shard_map(body, mesh=mesh, in_specs=in_specs, out_specs=out_specs, check_vma=False)
```

```python
import jax
import jax.numpy as jnp
from jax import lax
from jax.experimental import pallas as pl
from jax.experimental.pallas import tpu as pltpu
from jax.sharding import PartitionSpec as P

BF16 = jnp.bfloat16
F32 = jnp.float32
MESH = pl.DeviceIdType.MESH
CHIPS = 32


def iota(shape, dim):
    return lax.broadcasted_iota(jnp.int32, shape, dim)


def dot(lhs, rhs):
    return jnp.dot(lhs, rhs, preferred_element_type=F32)


def dot_turned(lhs, rhs):
    return lax.dot_general(lhs, rhs, (((1,), (1,)), ((), ())), preferred_element_type=F32)


def column_of(row):
    n = row.shape[1]
    eye = iota((n, n), 0) == iota((n, n), 1)
    return jnp.sum(jnp.where(eye, row, 0.0), axis=1, keepdims=True)


def neighbours(field):
    lanes = field.shape[1]
    lane = iota(field.shape, 1)
    below = jnp.where(lane == 0, 0.0, pltpu.roll(field, 1, 1))
    above = jnp.where(lane == lanes - 1, 0.0, pltpu.roll(field, lanes - 1, 1))
    return below, field, above


def relu_plus(summed, offset, channels, low=0, high=0, keep_low=None, keep_high=None):
    rows, lanes = summed.shape
    count = rows // channels
    parts = jnp.maximum(summed.reshape(count, channels, lanes) + offset[None], 0.0)
    if low or high:
        pieces = []
        if low:
            pieces.append(parts[:low] * keep_low)
        pieces.append(parts[low : count - high])
        if high:
            pieces.append(parts[count - high :] * keep_high)
        parts = jnp.concatenate([piece for piece in pieces if piece.shape[0]], axis=0)
    return parts.reshape(rows, lanes)


def gather_rows(summed, channels):
    rows, lanes = summed.shape
    taps = summed.reshape(rows // (3 * channels), 3, channels, lanes)
    below, here, above = (taps[:, b].reshape(rows // 3, lanes) for b in range(3))
    lane = iota((rows // 3, 128), 1)
    parts = []
    for n in range(lanes // 128):
        block = slice(128 * n, 128 * n + 128)
        parts.append(
            here[:, block]
            + jnp.where(lane == 0, 0.0, pltpu.roll(below[:, block], 1, 1))
            + jnp.where(lane == 127, 0.0, pltpu.roll(above[:, block], 127, 1))
        )
    return jnp.concatenate(parts, axis=1)


def widen(piece):
    rows, lanes = piece.shape
    return jnp.concatenate([piece.astype(F32), jnp.zeros((rows, 128 - lanes), F32)], axis=1)


def plane_band(weight_ref, band_ref):
    lane = iota((32, 128), 1)
    tiles = [[None] * 5 for _ in range(4)]
    for b in range(3):
        pieces = [widen(weight_ref[3 * a + b]) for a in range(3)]
        base = pieces[0] + pltpu.roll(pieces[1], 32, 1) + pltpu.roll(pieces[2], 64, 1)
        for m in range(4):
            start = 192 * b + 32 * m
            at, off = start // 128, start % 128
            moved = pltpu.roll(base, off, 1) if off else base
            shares = [(at, moved)]
            if off + 96 > 128:
                shares = [(at, jnp.where(lane >= off, moved, 0.0)), (at + 1, jnp.where(lane < off - 32, moved, 0.0))]
            for tile, share in shares:
                old = tiles[m][tile]
                tiles[m][tile] = share if old is None else old + share
    zero = jnp.zeros((32, 128), F32)
    for m in range(4):
        row = [zero if tile is None else tile for tile in tiles[m]]
        band_ref[32 * m : 32 * m + 32, :] = jnp.concatenate(row, axis=1)[:, 0:576].astype(BF16)


def kernel(
    image_hbm, crack_hbm, fold_hbm,
    w1_hbm, b1_hbm, w2_hbm, b2_hbm, wm_hbm, bm_hbm, wd_hbm, bd_hbm, wl_hbm, bl_hbm, wc_hbm, bc_hbm, wh_hbm, bh_hbm,
    out_ref,
    image_ref, crack_ref, fold_ref,
    w1_ref, b1_ref, w2_ref, b2_ref, wm_ref, bm_ref, wd_ref, bd_ref, wl_ref, bl_ref, wc_ref, bc_ref, wh_ref, bh_ref,
    load_sem, swap_send, swap_recv, far_send, far_recv, pass_send, pass_recv,
    half, tile, strip,
    t1, t2, tm, td, tc, tl, th,
    vol, one, two, joined, pooled, mid, deep, dec,
):
    gz = lax.axis_index("gz")
    xy = lax.axis_index("xy")
    core = lax.rem(xy, 2)
    chip = lax.div(xy, 2)
    last_xy = lax.axis_size("xy") - 1
    keep_low = jnp.where(xy == 0, 0.0, 1.0)
    keep_high = jnp.where(xy == last_xy, 0.0, 1.0)
    twin = (gz, xy + 1 - 2 * core)

    x, y, z = lax.div(chip, 16), lax.rem(lax.div(chip, 4), 4), lax.rem(chip, 4)
    steps = [(i, j, k) for i in range(2) for j in range(4) for k in range(4)]
    steps.sort(key=lambda step: -(2 - abs(2 - step[1]) + 2 - abs(2 - step[2])))
    others = [16 * lax.rem(x + i, 2) + 4 * lax.rem(y + j, 4) + lax.rem(z + k, 4) for i, j, k in steps]

    sources = (
        image_hbm, crack_hbm, fold_hbm,
        w1_hbm, b1_hbm, w2_hbm, b2_hbm, wm_hbm, bm_hbm, wd_hbm, bd_hbm, wl_hbm, bl_hbm, wc_hbm, bc_hbm, wh_hbm, bh_hbm,
    )
    targets = (
        image_ref, crack_ref, fold_ref,
        w1_ref, b1_ref, w2_ref, b2_ref, wm_ref, bm_ref, wd_ref, bd_ref, wl_ref, bl_ref, wc_ref, bc_ref, wh_ref, bh_ref,
    )
    loads = [pltpu.make_async_copy(s, t, load_sem.at[i]) for i, (s, t) in enumerate(zip(sources, targets))]
    for load in loads:
        load.start()

    barrier = pltpu.get_barrier_semaphore()
    pl.semaphore_signal(barrier, inc=1, device_id=twin, device_id_type=MESH)
    source_gz = jnp.where(core == 1, gz, 1 - gz)
    target_gz = jnp.where(core == 0, gz, 1 - gz)

    for other in others:
        pl.semaphore_signal(barrier, inc=1, device_id=(source_gz, 2 * other + 1 - core), device_id_type=MESH)

    for load in loads[:3]:
        load.wait()
    keep = ((1 - crack_ref[...]) * (1 - fold_ref[...])).astype(F32)
    gated = image_ref[...].astype(F32) * keep
    gated = jnp.concatenate([gated[0], gated[1]], axis=0)
    half[core] = jnp.concatenate([gated[:, :1024], gated[:, 1024:]], axis=0).astype(BF16)

    pl.semaphore_wait(barrier, CHIPS + 1)
    swap = pltpu.make_async_remote_copy(
        src_ref=half.at[core], dst_ref=half.at[core], send_sem=swap_send, recv_sem=swap_recv,
        device_id=twin, device_id_type=MESH,
    )
    swap.start()
    swap.wait()

    sub = iota((8, 128), 0)
    lane = iota((8, 128), 1)
    bands = (half[0].astype(F32), half[1].astype(F32))
    moved = []
    for q in range(2):
        evens, odds = [], []
        for k in range(16):
            rows = slice(8 * (k // 8), 8 * (k // 8) + 8)
            lanes = slice(128 * (k % 8), 128 * (k % 8) + 128)
            low, high = bands[0][rows, lanes], bands[1][rows, lanes]
            if q == 0:
                both = jnp.where(sub < 4, low, pltpu.roll(high, 4, 0))
            else:
                both = jnp.where(sub < 4, pltpu.roll(low, 4, 0), high)
            evens.append(pltpu.roll(both, 16, 1))
            odds.append(pltpu.roll(both, 80, 1))
        moved.append((evens, odds))
    for k in range(16):
        even = [jnp.where(lane >= 16, moved[q][0][k], moved[q][0][max(k - 1, 0)]) for q in range(2)]
        odd = [jnp.where(lane < 80, moved[q][1][k], moved[q][1][min(k + 1, 15)]) for q in range(2)]
        tile[2 * k] = jnp.concatenate(even, axis=0).astype(BF16)
        tile[2 * k + 1] = jnp.concatenate(odd, axis=0).astype(BF16)

    for other in others:
        pltpu.make_async_remote_copy(
            src_ref=tile.at[other], dst_ref=strip.at[0, chip], send_sem=far_send, recv_sem=far_recv,
            device_id=(target_gz, 2 * other + 1 - core), device_id_type=MESH,
        ).start()

    for load in loads[3:]:
        load.wait()
    base = [jnp.zeros((32, 128), F32), jnp.zeros((32, 128), F32)]
    lane = iota((32, 128), 1)
    w1 = w1_ref[...].astype(F32)
    for a in range(3):
        for b in range(3):
            col = column_of(w1[3 * a + b : 3 * a + b + 1])
            base[b // 2] = jnp.where(lane == 64 * (b % 2) + a, col, base[b // 2])
    for i in range(46):
        for n in range(2):
            t1[32 * i : 32 * i + 32, 128 * n : 128 * n + 128] = pltpu.roll(base[n], i, 1).astype(BF16)

    plane_band(w2_ref, t2)
    plane_band(wc_ref, tc)

    eye = (iota((64, 64), 0) == iota((64, 64), 1)).astype(BF16)
    for e in range(3):
        place = jnp.where(gz == 0, e, 2 - e)
        for b in range(3):
            rows = [wm_ref[9 * place + 3 * a + b] for a in range(3)]
            base = dot_turned(eye, jnp.concatenate([*rows, jnp.zeros((32, 64), BF16)], axis=0))
            for m in range(2):
                moved = pltpu.roll(base, 32, 1) if m else base
                start = 192 * m + 64 * b
                tm[start : start + 64, 128 * e : 128 * e + 128] = moved.astype(BF16)
            pieces = [widen(wd_ref[9 * place + 3 * a + b]) for a in range(3)]
            turned = [pltpu.roll(piece, 64, 1) for piece in pieces]
            rows = ((pieces[0] + turned[1], pieces[2]), (turned[0], pieces[1] + turned[2]))
            for m in range(2):
                start = 192 * m + 64 * b
                for n in range(2):
                    td[start : start + 64, 256 * e + 128 * n : 256 * e + 128 * n + 128] = rows[m][n].astype(BF16)

    lift = widen(wl_ref[...])
    turned = pltpu.roll(lift, 64, 1)
    blank = jnp.zeros((32, 128), F32)
    for m in range(4):
        piece = turned if m % 2 else lift
        row = [piece, blank] if m < 2 else [blank, piece]
        tl[32 * m : 32 * m + 32, :] = jnp.concatenate(row, axis=1).astype(BF16)
    pick = (iota((32, 256), 0) == lax.rem(iota((32, 256), 1), 32)).astype(BF16)
    wide = dot(wh_ref[...], pick)
    row = iota((24, 256), 0)
    lane = iota((24, 256), 1)
    heads = jnp.zeros((24, 256), F32)
    for k in range(3):
        here = (row // 8 == k) & (row % 8 == lane // 32)
        heads = jnp.where(here, wide[k : k + 1], heads)
    th[...] = heads.astype(BF16)

    b1 = column_of(b1_ref[...])
    b2 = column_of(b2_ref[...])
    bm = column_of(bm_ref[...])
    bd = column_of(bd_ref[...])
    bl = column_of(bl_ref[...])
    bc = column_of(bc_ref[...])
    hrow = iota((24, 1), 0)
    bh_row = bh_ref[...]
    bh = jnp.where(hrow < 8, bh_row[:, 0:1], jnp.where(hrow < 16, bh_row[:, 1:2], bh_row[:, 2:3]))

    pltpu.make_async_copy(strip.at[0], strip.at[0], far_recv).wait()
    hand = pltpu.make_async_remote_copy(
        src_ref=strip.at[0], dst_ref=strip.at[1], send_sem=pass_send, recv_sem=pass_recv,
        device_id=twin, device_id_type=MESH,
    )
    hand.start()

    u = iota((64, 128), 0)
    l = iota((64, 128), 1)
    place = 32 * xy - 8 + u
    inside = (u < 48) & (place >= 0) & (place < 32 * (last_xy + 1))
    select = jnp.where(inside & (l == 8 + 32 * core + u), 1.0, 0.0).astype(BF16)

    for source in range(2):
        if source == 1:
            hand.wait()
        tiles = strip[source].astype(F32).reshape(CHIPS, 2, 8, 128)
        for q in range(2):
            p = 2 * source + q
            rows = tiles[:, q].reshape(256, 128).astype(BF16)
            turned = dot_turned(select, rows)
            for b, part in enumerate(neighbours(turned)):
                vol[p, 64 * b : 64 * b + 64, :] = part.astype(BF16)
            for chunk in range(2):
                rows = slice(736 * chunk, 736 * chunk + 736)
                found = dot(t1[rows, 0:192], vol[p])
                if chunk == 0:
                    found = relu_plus(found, b1, 32, low=7, keep_low=keep_low)
                else:
                    found = relu_plus(found, b1, 32, high=7, keep_high=keep_high)
                for b, part in enumerate(neighbours(found)):
                    one[p, b, rows, :] = part.astype(BF16)
        for g in range(11):
            for q in range(2):
                p = 2 * source + q
                field = jnp.concatenate([one[p, b, 128 * g : 128 * g + 192, :] for b in range(3)], axis=0)
                found = relu_plus(dot(t2[...], field), b2, 32)
                two[p, 128 * g : 128 * g + 128, :] = found.astype(BF16)
                pairs = found.reshape(2, 2, 32, 256)
                pairs = jnp.maximum(pairs[:, 0], pairs[:, 1]).reshape(64, 256)
                pairs = jnp.maximum(pairs, pltpu.roll(pairs, 255, 1))
                joined[p, 64 * g : 64 * g + 64, :] = pairs.astype(BF16)

    fine = iota((256, 128), 0)
    coarse = iota((256, 128), 1)
    pick = jnp.where(fine == 2 * coarse, 1.0, 0.0).astype(BF16)
    pooled[:, 0:128] = jnp.zeros((704, 128), BF16)
    for p in range(4):
        found = dot(joined[p], pick)
        found = jnp.concatenate([found[:96] * keep_low, found[96:608], found[608:] * keep_high], axis=0).astype(BF16)
        t = jnp.where(core == 1, 2 * (p // 2), 2 - 2 * (p // 2)) + jnp.where(gz == 0, p % 2, 1 - p % 2)
        pooled[:, pl.ds(pl.multiple_of(128 * (t + 1), 128), 128)] = found

    mid[:, 0:128] = jnp.zeros((1280, 128), BF16)
    for g in range(5):
        field = []
        for e in range(3):
            near = [pooled[128 * g + 64 * h : 128 * g + 64 * h + 128, 128 * e : 128 * e + 384] for h in range(2)]
            field.append(jnp.concatenate([near[0][:, :256], near[1][:, :256], near[0][:, 256:], near[1][:, 256:]], axis=1))
        found = gather_rows(dot(tm[...], jnp.concatenate(field, axis=0)), 64)
        found = jnp.maximum(found.reshape(2, 64, 768) + bm[None], 0.0).reshape(128, 768)
        for h in range(2):
            part = jnp.concatenate([found[:, 256 * h : 256 * h + 256], found[:, 512 + 128 * h : 640 + 128 * h]], axis=1)
            if g == 0 and h == 0:
                part = part * keep_low
            if g == 4 and h == 1:
                part = part * keep_high
            mid[256 * g + 128 * h : 256 * g + 128 * h + 128, 128:512] = part.astype(BF16)

    for g in range(9):
        field = jnp.concatenate([mid[128 * g : 128 * g + 256, 128 * e : 128 * e + 256] for e in range(3)], axis=0)
        found = gather_rows(dot(td[...], field), 64)
        deep[128 * g : 128 * g + 128, :] = jnp.maximum(found.reshape(2, 64, 256) + bd[None], 0.0).reshape(128, 256).astype(BF16)

    fine = iota((256, 256), 1)
    coarse = iota((256, 256), 0)
    double = jnp.where(fine // 2 == coarse % 128, 1.0, 0.0).astype(BF16)
    for g in range(5):
        count = 4 if g < 4 else 2
        rows = dot(tl[0 : 32 * count, 0 : 64 * count], deep[256 * g : 256 * g + 64 * count, :])
        rows = (rows.reshape(count, 32, 256) + bl[None]).reshape(32 * count, 256)
        high = rows.astype(BF16)
        low = (rows - high.astype(F32)).astype(BF16)
        for t in range(2):
            both = jnp.concatenate([high[:, 128 * t : 128 * t + 128], low[:, 128 * t : 128 * t + 128]], axis=1)
            lifted = dot(both, double)
            for r in range(count):
                for p in range(2):
                    v = 2 * (4 * g + r) + p
                    p = jnp.where(core == 1, 0, 2) + jnp.where(gz == 0, t, 1 - t)
                    old = two[p, 32 * (v + 4) : 32 * (v + 5), :].astype(F32)
                    found = jnp.maximum(lifted[32 * r : 32 * r + 32] + old, 0.0)
                    if v < 2:
                        found = found * keep_low
                    if v >= 34:
                        found = found * keep_high
                    for b, part in enumerate(neighbours(found)):
                        dec[t, b, 32 * v : 32 * v + 32, :] = part.astype(BF16)

    for g in range(4):
        for t in range(2):
            parts = []
            for h in range(2):
                start = g * 256 + 128 * h + 32
                field = jnp.concatenate([dec[t, b, start : start + 192, :] for b in range(3)], axis=0)
                parts.append(relu_plus(dot(tc[...], field), bc, 32).astype(BF16))
            logits = dot(th[...], jnp.concatenate(parts, axis=0)) + bh
            found = jax.nn.sigmoid(logits)
            s = jnp.where(gz == 0, t, 1 - t)
            for k in range(3):
                out_ref[k, s, 8 * g : 8 * g + 8, :] = found[8 * k : 8 * k + 8]

    pltpu.make_async_copy(tile, tile, far_send).wait()


def body(image, crack, fold, *weights):
    rows = [weight[None] if weight.ndim == 1 else weight for weight in weights]
    rows[4] = jnp.swapaxes(rows[4], 1, 2)
    operands = (image, crack, fold, *rows)
    dma = pltpu.SemaphoreType.DMA
    scratch = [pltpu.VMEM(operand.shape, operand.dtype) for operand in operands]
    scratch += [dma((len(operands),)), dma, dma, dma, dma, dma, dma]
    scratch += [
        pltpu.VMEM(shape, BF16)
        for shape in (
            (2, 16, 1024), (CHIPS, 16, 128), (2, CHIPS, 16, 128),
            (1472, 256), (128, 576), (384, 384), (384, 768), (128, 576), (128, 256), (24, 256),
            (4, 192, 256), (4, 3, 1472, 256), (4, 1408, 256), (4, 704, 256), (704, 640), (1280, 512),
            (1152, 256), (2, 3, 1152, 256),
        )
    ]
    return pl.pallas_call(
        kernel,
        out_shape=pltpu.VMEM((3, 2, 32, 256), F32),
        in_specs=[pl.BlockSpec(memory_space=pl.ANY)] * len(operands),
        out_specs=pl.BlockSpec(memory_space=pltpu.VMEM),
        scratch_shapes=scratch,
        compiler_params=pltpu.CompilerParams(
            collective_id=0, has_side_effects=True, vmem_limit_bytes=60 * 1024 * 1024
        ),
        name="window",
    )(*operands)


def solution(mesh):
    in_specs = (P("gz", "xy", None),) * 3 + (P(),) * 14
    out_specs = P(None, "gz", "xy", None)
    return jax.shard_map(body, mesh=mesh, in_specs=in_specs, out_specs=out_specs, check_vma=False)
```

```python
import jax
import jax.numpy as jnp
from jax import lax
from jax.experimental import pallas as pl
from jax.experimental.pallas import tpu as pltpu
from jax.sharding import PartitionSpec as P

BF16 = jnp.bfloat16
F32 = jnp.float32
MESH = pl.DeviceIdType.MESH
CHIPS = 32


def iota(shape, dim):
    return lax.broadcasted_iota(jnp.int32, shape, dim)


def dot(lhs, rhs):
    return jnp.dot(lhs, rhs, preferred_element_type=F32)


def dot_turned(lhs, rhs):
    return lax.dot_general(lhs, rhs, (((1,), (1,)), ((), ())), preferred_element_type=F32)


def column_of(row):
    n = row.shape[1]
    eye = iota((n, n), 0) == iota((n, n), 1)
    return jnp.sum(jnp.where(eye, row, 0.0), axis=1, keepdims=True)


def neighbours(field):
    lanes = field.shape[1]
    lane = iota(field.shape, 1)
    below = jnp.where(lane == 0, 0.0, pltpu.roll(field, 1, 1))
    above = jnp.where(lane == lanes - 1, 0.0, pltpu.roll(field, lanes - 1, 1))
    return below, field, above


def relu_plus(summed, offset, channels, low=0, high=0, keep_low=None, keep_high=None):
    rows, lanes = summed.shape
    count = rows // channels
    parts = jnp.maximum(summed.reshape(count, channels, lanes) + offset[None], 0.0)
    if low or high:
        pieces = []
        if low:
            pieces.append(parts[:low] * keep_low)
        pieces.append(parts[low : count - high])
        if high:
            pieces.append(parts[count - high :] * keep_high)
        parts = jnp.concatenate([piece for piece in pieces if piece.shape[0]], axis=0)
    return parts.reshape(rows, lanes)


def gather_rows(summed, channels):
    rows, lanes = summed.shape
    taps = summed.reshape(rows // (3 * channels), 3, channels, lanes)
    below, here, above = (taps[:, b].reshape(rows // 3, lanes) for b in range(3))
    lane = iota((rows // 3, 128), 1)
    parts = []
    for n in range(lanes // 128):
        block = slice(128 * n, 128 * n + 128)
        parts.append(
            here[:, block]
            + jnp.where(lane == 0, 0.0, pltpu.roll(below[:, block], 1, 1))
            + jnp.where(lane == 127, 0.0, pltpu.roll(above[:, block], 127, 1))
        )
    return jnp.concatenate(parts, axis=1)


def widen(piece):
    rows, lanes = piece.shape
    return jnp.concatenate([piece.astype(F32), jnp.zeros((rows, 128 - lanes), F32)], axis=1)


def plane_band(weight_ref, band_ref):
    lane = iota((32, 128), 1)
    tiles = [[None] * 5 for _ in range(4)]
    for b in range(3):
        pieces = [widen(weight_ref[3 * a + b]) for a in range(3)]
        base = pieces[0] + pltpu.roll(pieces[1], 32, 1) + pltpu.roll(pieces[2], 64, 1)
        for m in range(4):
            start = 192 * b + 32 * m
            at, off = start // 128, start % 128
            moved = pltpu.roll(base, off, 1) if off else base
            shares = [(at, moved)]
            if off + 96 > 128:
                shares = [(at, jnp.where(lane >= off, moved, 0.0)), (at + 1, jnp.where(lane < off - 32, moved, 0.0))]
            for tile, share in shares:
                old = tiles[m][tile]
                tiles[m][tile] = share if old is None else old + share
    zero = jnp.zeros((32, 128), F32)
    for m in range(4):
        row = [zero if tile is None else tile for tile in tiles[m]]
        band_ref[32 * m : 32 * m + 32, :] = jnp.concatenate(row, axis=1)[:, 0:576].astype(BF16)


def kernel(
    image_hbm, crack_hbm, fold_hbm,
    w1_hbm, b1_hbm, w2_hbm, b2_hbm, wm_hbm, bm_hbm, wd_hbm, bd_hbm, wl_hbm, bl_hbm, wc_hbm, bc_hbm, wh_hbm, bh_hbm,
    out_ref,
    image_ref, crack_ref, fold_ref,
    w1_ref, b1_ref, w2_ref, b2_ref, wm_ref, bm_ref, wd_ref, bd_ref, wl_ref, bl_ref, wc_ref, bc_ref, wh_ref, bh_ref,
    load_sem, swap_send, swap_recv, far_send, far_recv, pass_send, pass_recv,
    half, tile, strip,
    t1, t2, tm, td, tc, tl, th,
    vol, one, two, joined, pooled, mid, deep, lifts, dec,
):
    gz = lax.axis_index("gz")
    xy = lax.axis_index("xy")
    core = lax.rem(xy, 2)
    chip = lax.div(xy, 2)
    last_xy = lax.axis_size("xy") - 1
    keep_low = jnp.where(xy == 0, 0.0, 1.0)
    keep_high = jnp.where(xy == last_xy, 0.0, 1.0)
    twin = (gz, xy + 1 - 2 * core)

    x, y, z = lax.div(chip, 16), lax.rem(lax.div(chip, 4), 4), lax.rem(chip, 4)
    steps = [(i, j, k) for i in range(2) for j in range(4) for k in range(4)]
    steps.sort(key=lambda step: -(2 - abs(2 - step[1]) + 2 - abs(2 - step[2])))
    others = [16 * lax.rem(x + i + 1 - core, 2) + 4 * lax.rem(y + j, 4) + lax.rem(z + k, 4) for i, j, k in steps]

    sources = (
        image_hbm, crack_hbm, fold_hbm,
        w1_hbm, b1_hbm, w2_hbm, b2_hbm, wm_hbm, bm_hbm, wd_hbm, bd_hbm, wl_hbm, bl_hbm, wc_hbm, bc_hbm, wh_hbm, bh_hbm,
    )
    targets = (
        image_ref, crack_ref, fold_ref,
        w1_ref, b1_ref, w2_ref, b2_ref, wm_ref, bm_ref, wd_ref, bd_ref, wl_ref, bl_ref, wc_ref, bc_ref, wh_ref, bh_ref,
    )
    loads = [pltpu.make_async_copy(s, t, load_sem.at[i]) for i, (s, t) in enumerate(zip(sources, targets))]
    for load in loads[:3]:
        load.start()

    barrier = pltpu.get_barrier_semaphore()
    pl.semaphore_signal(barrier, inc=1, device_id=twin, device_id_type=MESH)
    source_gz = jnp.where(core == 1, gz, 1 - gz)
    target_gz = jnp.where(core == 0, gz, 1 - gz)

    for other in others:
        pl.semaphore_signal(barrier, inc=1, device_id=(source_gz, 2 * other + 1 - core), device_id_type=MESH)

    for load in loads[:3]:
        load.wait()
    keep = ((1 - crack_ref[...]) * (1 - fold_ref[...])).astype(F32)
    gated = image_ref[...].astype(F32) * keep
    gated = jnp.concatenate([gated[0], gated[1]], axis=0)
    half[core] = jnp.concatenate([gated[:, :1024], gated[:, 1024:]], axis=0).astype(BF16)

    pl.semaphore_wait(barrier, CHIPS + 1)
    swap = pltpu.make_async_remote_copy(
        src_ref=half.at[core], dst_ref=half.at[core], send_sem=swap_send, recv_sem=swap_recv,
        device_id=twin, device_id_type=MESH,
    )
    swap.start()
    for load in loads[3:]:
        load.start()
    swap.wait()

    sub = iota((8, 128), 0)
    lane = iota((8, 128), 1)
    bands = (half[0].astype(F32), half[1].astype(F32))
    moved = []
    for q in range(2):
        evens, odds = [], []
        for k in range(16):
            rows = slice(8 * (k // 8), 8 * (k // 8) + 8)
            lanes = slice(128 * (k % 8), 128 * (k % 8) + 128)
            low, high = bands[0][rows, lanes], bands[1][rows, lanes]
            if q == 0:
                both = jnp.where(sub < 4, low, pltpu.roll(high, 4, 0))
            else:
                both = jnp.where(sub < 4, pltpu.roll(low, 4, 0), high)
            evens.append(pltpu.roll(both, 16, 1))
            odds.append(pltpu.roll(both, 80, 1))
        moved.append((evens, odds))
    for k in range(16):
        even = [jnp.where(lane >= 16, moved[q][0][k], moved[q][0][max(k - 1, 0)]) for q in range(2)]
        odd = [jnp.where(lane < 80, moved[q][1][k], moved[q][1][min(k + 1, 15)]) for q in range(2)]
        tile[2 * k] = jnp.concatenate(even, axis=0).astype(BF16)
        tile[2 * k + 1] = jnp.concatenate(odd, axis=0).astype(BF16)

    for other in others:
        pltpu.make_async_remote_copy(
            src_ref=tile.at[other], dst_ref=strip.at[0, chip], send_sem=far_send, recv_sem=far_recv,
            device_id=(target_gz, 2 * other + 1 - core), device_id_type=MESH,
        ).start()

    for load in loads[3:]:
        load.wait()
    base = [jnp.zeros((32, 128), F32), jnp.zeros((32, 128), F32)]
    lane = iota((32, 128), 1)
    w1 = w1_ref[...].astype(F32)
    for a in range(3):
        for b in range(3):
            col = column_of(w1[3 * a + b : 3 * a + b + 1])
            base[b // 2] = jnp.where(lane == 64 * (b % 2) + a, col, base[b // 2])
    for i in range(46):
        for n in range(2):
            t1[32 * i : 32 * i + 32, 128 * n : 128 * n + 128] = pltpu.roll(base[n], i, 1).astype(BF16)

    plane_band(w2_ref, t2)
    plane_band(wc_ref, tc)

    eye = (iota((64, 64), 0) == iota((64, 64), 1)).astype(BF16)
    for e in range(3):
        place = jnp.where(gz == 0, e, 2 - e)
        for b in range(3):
            rows = [wm_ref[9 * place + 3 * a + b] for a in range(3)]
            base = dot_turned(eye, jnp.concatenate([*rows, jnp.zeros((32, 64), BF16)], axis=0))
            for m in range(2):
                moved = pltpu.roll(base, 32, 1) if m else base
                start = 192 * m + 64 * b
                tm[start : start + 64, 128 * e : 128 * e + 128] = moved.astype(BF16)
            pieces = [widen(wd_ref[9 * place + 3 * a + b]) for a in range(3)]
            turned = [pltpu.roll(piece, 64, 1) for piece in pieces]
            rows = ((pieces[0] + turned[1], pieces[2]), (turned[0], pieces[1] + turned[2]))
            for m in range(2):
                start = 192 * m + 64 * b
                for n in range(2):
                    td[start : start + 64, 256 * e + 128 * n : 256 * e + 128 * n + 128] = rows[m][n].astype(BF16)

    lift = widen(wl_ref[...])
    turned = pltpu.roll(lift, 64, 1)
    blank = jnp.zeros((32, 128), F32)
    for m in range(4):
        piece = turned if m % 2 else lift
        row = [piece, blank] if m < 2 else [blank, piece]
        tl[32 * m : 32 * m + 32, :] = jnp.concatenate(row, axis=1).astype(BF16)
    pick = (iota((32, 256), 0) == lax.rem(iota((32, 256), 1), 32)).astype(BF16)
    wide = dot(wh_ref[...], pick)
    row = iota((24, 256), 0)
    lane = iota((24, 256), 1)
    heads = jnp.zeros((24, 256), F32)
    for k in range(3):
        here = (row // 8 == k) & (row % 8 == lane // 32)
        heads = jnp.where(here, wide[k : k + 1], heads)
    th[...] = heads.astype(BF16)

    b1 = column_of(b1_ref[...])
    b2 = column_of(b2_ref[...])
    bm = column_of(bm_ref[...])
    bd = column_of(bd_ref[...])
    bl = column_of(bl_ref[...])
    bc = column_of(bc_ref[...])
    hrow = iota((24, 1), 0)
    bh_row = bh_ref[...]
    bh = jnp.where(hrow < 8, bh_row[:, 0:1], jnp.where(hrow < 16, bh_row[:, 1:2], bh_row[:, 2:3]))

    pltpu.make_async_copy(strip.at[0], strip.at[0], far_recv).wait()
    hand = pltpu.make_async_remote_copy(
        src_ref=strip.at[0], dst_ref=strip.at[1], send_sem=pass_send, recv_sem=pass_recv,
        device_id=twin, device_id_type=MESH,
    )
    hand.start()

    u = iota((64, 128), 0)
    l = iota((64, 128), 1)
    place = 32 * xy - 8 + u
    inside = (u < 48) & (place >= 0) & (place < 32 * (last_xy + 1))
    select = jnp.where(inside & (l == 8 + 32 * core + u), 1.0, 0.0).astype(BF16)

    for source in range(2):
        if source == 1:
            hand.wait()
        tiles = strip[source].astype(F32).reshape(CHIPS, 2, 8, 128)
        for q in range(2):
            p = 2 * source + q
            rows = tiles[:, q].reshape(256, 128).astype(BF16)
            turned = dot_turned(select, rows)
            for b, part in enumerate(neighbours(turned)):
                vol[p, 64 * b : 64 * b + 64, :] = part.astype(BF16)
            for chunk in range(2):
                rows = slice(736 * chunk, 736 * chunk + 736)
                found = dot(t1[rows, 0:192], vol[p])
                if chunk == 0:
                    found = relu_plus(found, b1, 32, low=7, keep_low=keep_low)
                else:
                    found = relu_plus(found, b1, 32, high=7, keep_high=keep_high)
                for b, part in enumerate(neighbours(found)):
                    one[p, b, rows, :] = part.astype(BF16)
        for g in range(11):
            for q in range(2):
                p = 2 * source + q
                field = jnp.concatenate([one[p, b, 128 * g : 128 * g + 192, :] for b in range(3)], axis=0)
                found = relu_plus(dot(t2[...], field), b2, 32)
                two[p, 128 * g : 128 * g + 128, :] = found.astype(BF16)
                pairs = found.reshape(2, 2, 32, 256)
                pairs = jnp.maximum(pairs[:, 0], pairs[:, 1]).reshape(64, 256)
                pairs = jnp.maximum(pairs, pltpu.roll(pairs, 255, 1))
                joined[p, 64 * g : 64 * g + 64, :] = pairs.astype(BF16)

    fine = iota((256, 128), 0)
    coarse = iota((256, 128), 1)
    pick = jnp.where(fine == 2 * coarse, 1.0, 0.0).astype(BF16)
    for p in range(4):
        found = dot(joined[p], pick)
        found = jnp.concatenate([found[:96] * keep_low, found[96:608], found[608:] * keep_high], axis=0).astype(BF16)
        t = jnp.where(core == 1, 2 * (p // 2), 2 - 2 * (p // 2)) + jnp.where(gz == 0, p % 2, 1 - p % 2)
        pooled[:, pl.ds(pl.multiple_of(128 * (t + 1), 128), 128)] = found

    mid[1024:1280, 0:128] = jnp.zeros((256, 128), BF16)
    for g in range(5):
        rows = [slice(128 * g + 64 * h, 128 * g + 64 * h + 128) for h in range(2)]
        field = [jnp.concatenate([pooled[rows[h], 128 * e : 128 * e + 128] for h in range(2)], axis=1) for e in (1, 2)]
        sums = [dot(tm[:, 128:384], jnp.concatenate(field, axis=0))]
        for h in range(2):
            field = [pooled[rows[h], 128 * e + 128 : 128 * e + 384] for e in range(3)]
            sums.append(dot(tm[...], jnp.concatenate(field, axis=0)))
        found = []
        for summed in sums:
            summed = gather_rows(summed, 64)
            found.append(jnp.maximum(summed.reshape(2, 64, 256) + bm[None], 0.0).reshape(128, 256))
        for h in range(2):
            scale = keep_low if g == 0 and h == 0 else keep_high if g == 4 and h == 1 else None
            start = 256 * g + 128 * h
            for part, lanes in ((found[0][:, 128 * h : 128 * h + 128], slice(128, 256)), (found[1 + h], slice(256, 512))):
                if scale is not None:
                    part = part * scale
                mid[start : start + 128, lanes] = part.astype(BF16)

    for g in range(0, 9, 2):
        rows = [slice(128 * i, 128 * i + 256) for i in (g, g + 1)]
        if g < 8:
            sums = []
            for t in range(2):
                field = [
                    jnp.concatenate([mid[row, 128 * (e + t) : 128 * (e + t) + 128] for row in rows], axis=1)
                    for e in range(1 - t, 3)
                ]
                sums.append(dot(td[:, 256 * (1 - t) : 768], jnp.concatenate(field, axis=0)))
        else:
            sums = [dot(td[...], jnp.concatenate([mid[rows[0], 128 * e : 128 * e + 256] for e in range(3)], axis=0))]
        found = []
        for summed in sums:
            summed = gather_rows(summed, 64)
            found.append(jnp.maximum(summed.reshape(2, 64, 256) + bd[None], 0.0).reshape(128, 256).astype(BF16))
        if g < 8:
            for i in range(2):
                start = 128 * (g + i)
                for t in range(2):
                    deep[start : start + 128, 128 * t : 128 * t + 128] = found[t][:, 128 * i : 128 * i + 128]
        else:
            deep[1024:1152, :] = found[0]

    for g in range(5):
        count = 4 if g < 4 else 2
        rows = dot(tl[0 : 32 * count, 0 : 64 * count], deep[256 * g : 256 * g + 64 * count, :])
        rows = (rows.reshape(count, 32, 256) + bl[None]).reshape(32 * count, 256)
        high = rows.astype(BF16)
        low = (rows - high.astype(F32)).astype(BF16)
        for t in range(2):
            both = jnp.concatenate([high[:, 128 * t : 128 * t + 128], low[:, 128 * t : 128 * t + 128]], axis=1)
            lifts[t, 128 * g : 128 * g + 32 * count, :] = both

    fine = iota((256, 256), 1)
    coarse = iota((256, 256), 0)
    double = jnp.where(fine // 2 == coarse % 128, 1.0, 0.0).astype(BF16)
    for g in range(5):
        count = 4 if g < 4 else 2
        for t in range(2):
            lifted = dot(lifts[t, 128 * g : 128 * g + 32 * count, :], double)
            p = jnp.where(core == 1, 0, 2) + jnp.where(gz == 0, t, 1 - t)
            for r in range(count):
                for q in range(2):
                    v = 2 * (4 * g + r) + q
                    old = two[p, 32 * (v + 4) : 32 * (v + 5), :].astype(F32)
                    found = jnp.maximum(lifted[32 * r : 32 * r + 32] + old, 0.0)
                    if v < 2:
                        found = found * keep_low
                    if v >= 34:
                        found = found * keep_high
                    for b, part in enumerate(neighbours(found)):
                        dec[t, b, 32 * v : 32 * v + 32, :] = part.astype(BF16)

    steps = [(g, t) for g in range(4) for t in range(2)]
    fields = []
    for step in range(len(steps) + 2):
        if step < len(steps):
            g, t = steps[step]
            parts = []
            for h in range(2):
                start = g * 256 + 128 * h + 32
                field = jnp.concatenate([dec[t, b, start : start + 192, :] for b in range(3)], axis=0)
                parts.append(relu_plus(dot(tc[...], field), bc, 32).astype(BF16))
            fields.append(jnp.concatenate(parts, axis=0))
        if step >= 2:
            g, t = steps[step - 2]
            found = jax.nn.sigmoid(dot(th[...], fields[step - 2]) + bh)
            s = jnp.where(gz == 0, t, 1 - t)
            for k in range(3):
                out_ref[k, s, 8 * g : 8 * g + 8, :] = found[8 * k : 8 * k + 8]

    pltpu.make_async_copy(tile, tile, far_send).wait()


def body(image, crack, fold, *weights):
    rows = [weight[None] if weight.ndim == 1 else weight for weight in weights]
    rows[4] = jnp.swapaxes(rows[4], 1, 2)
    operands = (image, crack, fold, *rows)
    dma = pltpu.SemaphoreType.DMA
    scratch = [pltpu.VMEM(operand.shape, operand.dtype) for operand in operands]
    scratch += [dma((len(operands),)), dma, dma, dma, dma, dma, dma]
    scratch += [
        pltpu.VMEM(shape, BF16)
        for shape in (
            (2, 16, 1024), (CHIPS, 16, 128), (2, CHIPS, 16, 128),
            (1472, 256), (128, 576), (384, 384), (384, 768), (128, 576), (128, 256), (24, 256),
            (4, 192, 256), (4, 3, 1472, 256), (4, 1408, 256), (4, 704, 256), (704, 640), (1280, 512),
            (1152, 256), (2, 576, 256), (2, 3, 1152, 256),
        )
    ]
    return pl.pallas_call(
        kernel,
        out_shape=pltpu.VMEM((3, 2, 32, 256), F32),
        in_specs=[pl.BlockSpec(memory_space=pl.ANY)] * len(operands),
        out_specs=pl.BlockSpec(memory_space=pltpu.VMEM),
        scratch_shapes=scratch,
        compiler_params=pltpu.CompilerParams(
            collective_id=0, has_side_effects=True, vmem_limit_bytes=60 * 1024 * 1024
        ),
        name="window",
    )(*operands)


def solution(mesh):
    in_specs = (P("gz", "xy", None),) * 3 + (P(),) * 14
    out_specs = P(None, "gz", "xy", None)
    return jax.shard_map(body, mesh=mesh, in_specs=in_specs, out_specs=out_specs, check_vma=False)
```

```python
import jax
import jax.numpy as jnp
from jax import lax
from jax.experimental import pallas as pl
from jax.experimental.pallas import tpu as pltpu
from jax.sharding import PartitionSpec as P

BF16 = jnp.bfloat16
F32 = jnp.float32
MESH = pl.DeviceIdType.MESH
CHIPS = 32


def iota(shape, dim):
    return lax.broadcasted_iota(jnp.int32, shape, dim)


def dot(lhs, rhs):
    return jnp.dot(lhs, rhs, preferred_element_type=F32)


def dot_turned(lhs, rhs):
    return lax.dot_general(lhs, rhs, (((1,), (1,)), ((), ())), preferred_element_type=F32)


def column_of(row):
    n = row.shape[1]
    eye = iota((n, n), 0) == iota((n, n), 1)
    return jnp.sum(jnp.where(eye, row, 0.0), axis=1, keepdims=True)


def neighbours(field):
    lanes = field.shape[1]
    lane = iota(field.shape, 1)
    below = jnp.where(lane == 0, 0.0, pltpu.roll(field, 1, 1))
    above = jnp.where(lane == lanes - 1, 0.0, pltpu.roll(field, lanes - 1, 1))
    return below, field, above


def relu_plus(summed, offset, channels, low=0, high=0, keep_low=None, keep_high=None):
    rows, lanes = summed.shape
    count = rows // channels
    parts = jnp.maximum(summed.reshape(count, channels, lanes) + offset[None], 0.0)
    if low or high:
        pieces = []
        if low:
            pieces.append(parts[:low] * keep_low)
        pieces.append(parts[low : count - high])
        if high:
            pieces.append(parts[count - high :] * keep_high)
        parts = jnp.concatenate([piece for piece in pieces if piece.shape[0]], axis=0)
    return parts.reshape(rows, lanes)


def gather_rows(summed, channels):
    rows, lanes = summed.shape
    taps = summed.reshape(rows // (3 * channels), 3, channels, lanes)
    below, here, above = (taps[:, b].reshape(rows // 3, lanes) for b in range(3))
    lane = iota((rows // 3, 128), 1)
    parts = []
    for n in range(lanes // 128):
        block = slice(128 * n, 128 * n + 128)
        parts.append(
            here[:, block]
            + jnp.where(lane == 0, 0.0, pltpu.roll(below[:, block], 1, 1))
            + jnp.where(lane == 127, 0.0, pltpu.roll(above[:, block], 127, 1))
        )
    return jnp.concatenate(parts, axis=1)


def widen(piece):
    rows, lanes = piece.shape
    return jnp.concatenate([piece.astype(F32), jnp.zeros((rows, 128 - lanes), F32)], axis=1)


def plane_band(weight_ref, band_ref):
    lane = iota((32, 128), 1)
    tiles = [[None] * 5 for _ in range(4)]
    for b in range(3):
        pieces = [widen(weight_ref[3 * a + b]) for a in range(3)]
        base = pieces[0] + pltpu.roll(pieces[1], 32, 1) + pltpu.roll(pieces[2], 64, 1)
        for m in range(4):
            start = 192 * b + 32 * m
            at, off = start // 128, start % 128
            moved = pltpu.roll(base, off, 1) if off else base
            shares = [(at, moved)]
            if off + 96 > 128:
                shares = [(at, jnp.where(lane >= off, moved, 0.0)), (at + 1, jnp.where(lane < off - 32, moved, 0.0))]
            for tile, share in shares:
                old = tiles[m][tile]
                tiles[m][tile] = share if old is None else old + share
    zero = jnp.zeros((32, 128), F32)
    for m in range(4):
        row = [zero if tile is None else tile for tile in tiles[m]]
        band_ref[32 * m : 32 * m + 32, :] = jnp.concatenate(row, axis=1)[:, 0:576].astype(BF16)


def kernel(
    image_hbm, crack_hbm, fold_hbm,
    w1_hbm, b1_hbm, w2_hbm, b2_hbm, wm_hbm, bm_hbm, wd_hbm, bd_hbm, wl_hbm, bl_hbm, wc_hbm, bc_hbm, wh_hbm, bh_hbm,
    out_ref,
    image_ref, crack_ref, fold_ref,
    w1_ref, b1_ref, w2_ref, b2_ref, wm_ref, bm_ref, wd_ref, bd_ref, wl_ref, bl_ref, wc_ref, bc_ref, wh_ref, bh_ref,
    load_sem, swap_send, swap_recv, far_send, far_recv, pass_send, pass_recv,
    half, tile, strip,
    t1, t2, tm, td, tc, tl, th,
    vol, one, two, joined, pooled, mid, deep, lifts, dec,
):
    gz = lax.axis_index("gz")
    xy = lax.axis_index("xy")
    core = lax.rem(xy, 2)
    chip = lax.div(xy, 2)
    last_xy = lax.axis_size("xy") - 1
    keep_low = jnp.where(xy == 0, 0.0, 1.0)
    keep_high = jnp.where(xy == last_xy, 0.0, 1.0)
    twin = (gz, xy + 1 - 2 * core)

    x, y, z = lax.div(chip, 16), lax.rem(lax.div(chip, 4), 4), lax.rem(chip, 4)
    steps = [(i, j, k) for i in range(2) for j in range(4) for k in range(4)]
    steps.sort(key=lambda step: -(2 - abs(2 - step[1]) + 2 - abs(2 - step[2])))
    others = [16 * lax.rem(x + i + 1 - core, 2) + 4 * lax.rem(y + j, 4) + lax.rem(z + k, 4) for i, j, k in steps]

    sources = (
        image_hbm, crack_hbm, fold_hbm,
        w1_hbm, b1_hbm, w2_hbm, b2_hbm, wm_hbm, bm_hbm, wd_hbm, bd_hbm, wl_hbm, bl_hbm, wc_hbm, bc_hbm, wh_hbm, bh_hbm,
    )
    targets = (
        image_ref, crack_ref, fold_ref,
        w1_ref, b1_ref, w2_ref, b2_ref, wm_ref, bm_ref, wd_ref, bd_ref, wl_ref, bl_ref, wc_ref, bc_ref, wh_ref, bh_ref,
    )
    loads = [pltpu.make_async_copy(s, t, load_sem.at[i]) for i, (s, t) in enumerate(zip(sources, targets))]
    for load in loads[:3]:
        load.start()

    barrier = pltpu.get_barrier_semaphore()
    pl.semaphore_signal(barrier, inc=1, device_id=twin, device_id_type=MESH)
    source_gz = jnp.where(core == 1, gz, 1 - gz)
    target_gz = jnp.where(core == 0, gz, 1 - gz)

    for other in others:
        pl.semaphore_signal(barrier, inc=1, device_id=(source_gz, 2 * other + 1 - core), device_id_type=MESH)

    for load in loads[:3]:
        load.wait()
    keep = ((1 - crack_ref[...]) * (1 - fold_ref[...])).astype(F32)
    gated = image_ref[...].astype(F32) * keep
    gated = jnp.concatenate([gated[0], gated[1]], axis=0)
    half[core] = jnp.concatenate([gated[:, :1024], gated[:, 1024:]], axis=0).astype(BF16)

    pl.semaphore_wait(barrier, CHIPS + 1)
    swap = pltpu.make_async_remote_copy(
        src_ref=half.at[core], dst_ref=half.at[core], send_sem=swap_send, recv_sem=swap_recv,
        device_id=twin, device_id_type=MESH,
    )
    swap.start()
    for load in loads[3:]:
        load.start()
    swap.wait()

    sub = iota((8, 128), 0)
    lane = iota((8, 128), 1)
    bands = (half[0].astype(F32), half[1].astype(F32))
    moved = []
    for q in range(2):
        evens, odds = [], []
        for k in range(16):
            rows = slice(8 * (k // 8), 8 * (k // 8) + 8)
            lanes = slice(128 * (k % 8), 128 * (k % 8) + 128)
            low, high = bands[0][rows, lanes], bands[1][rows, lanes]
            if q == 0:
                both = jnp.where(sub < 4, low, pltpu.roll(high, 4, 0))
            else:
                both = jnp.where(sub < 4, pltpu.roll(low, 4, 0), high)
            evens.append(pltpu.roll(both, 16, 1))
            odds.append(pltpu.roll(both, 80, 1))
        moved.append((evens, odds))
    for k in range(16):
        even = [jnp.where(lane >= 16, moved[q][0][k], moved[q][0][max(k - 1, 0)]) for q in range(2)]
        odd = [jnp.where(lane < 80, moved[q][1][k], moved[q][1][min(k + 1, 15)]) for q in range(2)]
        tile[2 * k] = jnp.concatenate(even, axis=0).astype(BF16)
        tile[2 * k + 1] = jnp.concatenate(odd, axis=0).astype(BF16)

    for other in others:
        pltpu.make_async_remote_copy(
            src_ref=tile.at[other], dst_ref=strip.at[0, chip], send_sem=far_send, recv_sem=far_recv,
            device_id=(target_gz, 2 * other + 1 - core), device_id_type=MESH,
        ).start()

    for load in loads[3:]:
        load.wait()
    base = [jnp.zeros((32, 128), F32), jnp.zeros((32, 128), F32)]
    lane = iota((32, 128), 1)
    w1 = w1_ref[...].astype(F32)
    for a in range(3):
        for b in range(3):
            col = column_of(w1[3 * a + b : 3 * a + b + 1])
            base[b // 2] = jnp.where(lane == 64 * (b % 2) + a, col, base[b // 2])
    for i in range(46):
        for n in range(2):
            t1[32 * i : 32 * i + 32, 128 * n : 128 * n + 128] = pltpu.roll(base[n], i, 1).astype(BF16)

    plane_band(w2_ref, t2)
    plane_band(wc_ref, tc)

    eye = (iota((64, 64), 0) == iota((64, 64), 1)).astype(BF16)
    for e in range(3):
        place = jnp.where(gz == 0, e, 2 - e)
        for b in range(3):
            rows = [wm_ref[9 * place + 3 * a + b] for a in range(3)]
            base = dot_turned(eye, jnp.concatenate([*rows, jnp.zeros((32, 64), BF16)], axis=0))
            for m in range(2):
                moved = pltpu.roll(base, 32, 1) if m else base
                start = 192 * m + 64 * b
                tm[start : start + 64, 128 * e : 128 * e + 128] = moved.astype(BF16)
            pieces = [widen(wd_ref[9 * place + 3 * a + b]) for a in range(3)]
            turned = [pltpu.roll(piece, 64, 1) for piece in pieces]
            rows = ((pieces[0] + turned[1], pieces[2]), (turned[0], pieces[1] + turned[2]))
            for m in range(2):
                start = 192 * m + 64 * b
                for n in range(2):
                    td[start : start + 64, 256 * e + 128 * n : 256 * e + 128 * n + 128] = rows[m][n].astype(BF16)

    lift = widen(wl_ref[...])
    turned = pltpu.roll(lift, 64, 1)
    blank = jnp.zeros((32, 128), F32)
    for m in range(4):
        piece = turned if m % 2 else lift
        row = [piece, blank] if m < 2 else [blank, piece]
        tl[32 * m : 32 * m + 32, :] = jnp.concatenate(row, axis=1).astype(BF16)
    pick = (iota((32, 256), 0) == lax.rem(iota((32, 256), 1), 32)).astype(BF16)
    wide = dot(wh_ref[...], pick)
    row = iota((24, 256), 0)
    lane = iota((24, 256), 1)
    heads = jnp.zeros((24, 256), F32)
    for k in range(3):
        here = (row // 8 == k) & (row % 8 == lane // 32)
        heads = jnp.where(here, wide[k : k + 1], heads)
    th[...] = heads.astype(BF16)

    b1 = column_of(b1_ref[...])
    b2 = column_of(b2_ref[...])
    bm = column_of(bm_ref[...])
    bd = column_of(bd_ref[...])
    bl = column_of(bl_ref[...])
    bc = column_of(bc_ref[...])
    hrow = iota((24, 1), 0)
    bh_row = bh_ref[...]
    bh = jnp.where(hrow < 8, bh_row[:, 0:1], jnp.where(hrow < 16, bh_row[:, 1:2], bh_row[:, 2:3]))

    pltpu.make_async_copy(strip.at[0], strip.at[0], far_recv).wait()
    hand = pltpu.make_async_remote_copy(
        src_ref=strip.at[0], dst_ref=strip.at[1], send_sem=pass_send, recv_sem=pass_recv,
        device_id=twin, device_id_type=MESH,
    )
    hand.start()

    u = iota((64, 128), 0)
    l = iota((64, 128), 1)
    place = 32 * xy - 8 + u
    inside = (u < 48) & (place >= 0) & (place < 32 * (last_xy + 1))
    select = jnp.where(inside & (l == 8 + 32 * core + u), 1.0, 0.0).astype(BF16)

    fine = iota((256, 128), 0)
    coarse = iota((256, 128), 1)
    pick = jnp.where(fine == 2 * coarse, 1.0, 0.0).astype(BF16)

    def turn(source):
        tiles = strip[source].astype(F32).reshape(CHIPS, 2, 8, 128)
        for q in range(2):
            turned = dot_turned(select, tiles[:, q].reshape(256, 128).astype(BF16))
            for b, part in enumerate(neighbours(turned)):
                vol[2 * source + q, 64 * b : 64 * b + 64, :] = part.astype(BF16)

    def first_layer(p, start, stop):
        rows = slice(32 * start, 32 * stop)
        low, high = max(0, min(stop, 7) - start), max(0, stop - max(start, 39))
        found = relu_plus(dot(t1[rows, 0:192], vol[p]), b1, 32, low, high, keep_low, keep_high)
        for b, part in enumerate(neighbours(found)):
            one[p, b, rows, :] = part.astype(BF16)

    def second_layer(p, g):
        field = jnp.concatenate([one[p, b, 128 * g : 128 * g + 192, :] for b in range(3)], axis=0)
        found = relu_plus(dot(t2[...], field), b2, 32)
        two[p, 128 * g : 128 * g + 128, :] = found.astype(BF16)
        pairs = found.reshape(2, 2, 32, 256)
        pairs = jnp.maximum(pairs[:, 0], pairs[:, 1]).reshape(64, 256)
        pairs = jnp.maximum(pairs, pltpu.roll(pairs, 255, 1))
        joined[p, 64 * g : 64 * g + 64, :] = pairs.astype(BF16)

    def pool(p):
        found = dot(joined[p], pick)
        found = jnp.concatenate([found[:96] * keep_low, found[96:608], found[608:] * keep_high], axis=0).astype(BF16)
        t = jnp.where(core == 1, 2 * (p // 2), 2 - 2 * (p // 2)) + jnp.where(gz == 0, p % 2, 1 - p % 2)
        pooled[:, pl.ds(pl.multiple_of(128 * (t + 1), 128), 128)] = found

    turn(0)
    first_layer(0, 0, 23)
    first_layer(0, 23, 46)
    for p in range(1, 5):
        for g in range(11):
            second_layer(p - 1, g)
            if p == 1 and g == 9:
                hand.wait()
                turn(1)
            if p < 4:
                first_layer(p, 4 * g, 4 * g + 4 if g < 10 else 46)
            if p > 1 and g == 2:
                pool(p - 2)
    pool(3)

    mid[1024:1280, 0:128] = jnp.zeros((256, 128), BF16)
    for g in range(5):
        rows = [slice(128 * g + 64 * h, 128 * g + 64 * h + 128) for h in range(2)]
        field = [jnp.concatenate([pooled[rows[h], 128 * e : 128 * e + 128] for h in range(2)], axis=1) for e in (1, 2)]
        sums = [dot(tm[:, 128:384], jnp.concatenate(field, axis=0))]
        for h in range(2):
            field = [pooled[rows[h], 128 * e + 128 : 128 * e + 384] for e in range(3)]
            sums.append(dot(tm[...], jnp.concatenate(field, axis=0)))
        found = []
        for summed in sums:
            summed = gather_rows(summed, 64)
            found.append(jnp.maximum(summed.reshape(2, 64, 256) + bm[None], 0.0).reshape(128, 256))
        for h in range(2):
            scale = keep_low if g == 0 and h == 0 else keep_high if g == 4 and h == 1 else None
            start = 256 * g + 128 * h
            for part, lanes in ((found[0][:, 128 * h : 128 * h + 128], slice(128, 256)), (found[1 + h], slice(256, 512))):
                if scale is not None:
                    part = part * scale
                mid[start : start + 128, lanes] = part.astype(BF16)

    for g in range(0, 9, 2):
        rows = [slice(128 * i, 128 * i + 256) for i in (g, g + 1)]
        if g < 8:
            sums = []
            for t in range(2):
                field = [
                    jnp.concatenate([mid[row, 128 * (e + t) : 128 * (e + t) + 128] for row in rows], axis=1)
                    for e in range(1 - t, 3)
                ]
                sums.append(dot(td[:, 256 * (1 - t) : 768], jnp.concatenate(field, axis=0)))
        else:
            sums = [dot(td[...], jnp.concatenate([mid[rows[0], 128 * e : 128 * e + 256] for e in range(3)], axis=0))]
        found = []
        for summed in sums:
            summed = gather_rows(summed, 64)
            found.append(jnp.maximum(summed.reshape(2, 64, 256) + bd[None], 0.0).reshape(128, 256).astype(BF16))
        if g < 8:
            for i in range(2):
                start = 128 * (g + i)
                for t in range(2):
                    deep[start : start + 128, 128 * t : 128 * t + 128] = found[t][:, 128 * i : 128 * i + 128]
        else:
            deep[1024:1152, :] = found[0]

    for g in range(5):
        count = 4 if g < 4 else 2
        rows = dot(tl[0 : 32 * count, 0 : 64 * count], deep[256 * g : 256 * g + 64 * count, :])
        rows = (rows.reshape(count, 32, 256) + bl[None]).reshape(32 * count, 256)
        high = rows.astype(BF16)
        low = (rows - high.astype(F32)).astype(BF16)
        for t in range(2):
            both = jnp.concatenate([high[:, 128 * t : 128 * t + 128], low[:, 128 * t : 128 * t + 128]], axis=1)
            lifts[t, 128 * g : 128 * g + 32 * count, :] = both

    fine = iota((256, 256), 1)
    coarse = iota((256, 256), 0)
    double = jnp.where(fine // 2 == coarse % 128, 1.0, 0.0).astype(BF16)
    for g in range(5):
        count = 4 if g < 4 else 2
        for t in range(2):
            lifted = dot(lifts[t, 128 * g : 128 * g + 32 * count, :], double)
            p = jnp.where(core == 1, 0, 2) + jnp.where(gz == 0, t, 1 - t)
            for r in range(count):
                for q in range(2):
                    v = 2 * (4 * g + r) + q
                    old = two[p, 32 * (v + 4) : 32 * (v + 5), :].astype(F32)
                    found = jnp.maximum(lifted[32 * r : 32 * r + 32] + old, 0.0)
                    if v < 2:
                        found = found * keep_low
                    if v >= 34:
                        found = found * keep_high
                    for b, part in enumerate(neighbours(found)):
                        dec[t, b, 32 * v : 32 * v + 32, :] = part.astype(BF16)

    steps = [(g, t) for g in range(4) for t in range(2)]
    fields = []
    for step in range(len(steps) + 8):
        if step < len(steps):
            g, t = steps[step]
            parts = []
            for h in range(2):
                start = g * 256 + 128 * h + 32
                field = jnp.concatenate([dec[t, b, start : start + 192, :] for b in range(3)], axis=0)
                parts.append(relu_plus(dot(tc[...], field), bc, 32).astype(BF16))
            fields.append(jnp.concatenate(parts, axis=0))
        if step >= 8:
            g, t = steps[step - 8]
            found = jax.nn.sigmoid(dot(th[...], fields[step - 8]) + bh)
            s = jnp.where(gz == 0, t, 1 - t)
            for k in range(3):
                out_ref[k, s, 8 * g : 8 * g + 8, :] = found[8 * k : 8 * k + 8]

    pltpu.make_async_copy(tile, tile, far_send).wait()


def body(image, crack, fold, *weights):
    rows = [weight[None] if weight.ndim == 1 else weight for weight in weights]
    rows[4] = jnp.swapaxes(rows[4], 1, 2)
    operands = (image, crack, fold, *rows)
    dma = pltpu.SemaphoreType.DMA
    scratch = [pltpu.VMEM(operand.shape, operand.dtype) for operand in operands]
    scratch += [dma((len(operands),)), dma, dma, dma, dma, dma, dma]
    scratch += [
        pltpu.VMEM(shape, BF16)
        for shape in (
            (2, 16, 1024), (CHIPS, 16, 128), (2, CHIPS, 16, 128),
            (1472, 256), (128, 576), (384, 384), (384, 768), (128, 576), (128, 256), (24, 256),
            (4, 192, 256), (4, 3, 1472, 256), (4, 1408, 256), (4, 704, 256), (704, 640), (1280, 512),
            (1152, 256), (2, 576, 256), (2, 3, 1152, 256),
        )
    ]
    return pl.pallas_call(
        kernel,
        out_shape=pltpu.VMEM((3, 2, 32, 256), F32),
        in_specs=[pl.BlockSpec(memory_space=pl.ANY)] * len(operands),
        out_specs=pl.BlockSpec(memory_space=pltpu.VMEM),
        scratch_shapes=scratch,
        compiler_params=pltpu.CompilerParams(
            collective_id=0, has_side_effects=True, vmem_limit_bytes=60 * 1024 * 1024
        ),
        name="window",
    )(*operands)


def solution(mesh):
    in_specs = (P("gz", "xy", None),) * 3 + (P(),) * 14
    out_specs = P(None, "gz", "xy", None)
    return jax.shard_map(body, mesh=mesh, in_specs=in_specs, out_specs=out_specs, check_vma=False)
```

```python
import jax
import jax.numpy as jnp
from jax import lax
from jax.experimental import pallas as pl
from jax.experimental.pallas import tpu as pltpu
from jax.sharding import PartitionSpec as P

BF16 = jnp.bfloat16
F32 = jnp.float32
MESH = pl.DeviceIdType.MESH
CHIPS = 32


def iota(shape, dim):
    return lax.broadcasted_iota(jnp.int32, shape, dim)


def dot(lhs, rhs):
    return jnp.dot(lhs, rhs, preferred_element_type=F32)


def dot_turned(lhs, rhs):
    return lax.dot_general(lhs, rhs, (((1,), (1,)), ((), ())), preferred_element_type=F32)


def column_of(row):
    n = row.shape[1]
    eye = iota((n, n), 0) == iota((n, n), 1)
    return jnp.sum(jnp.where(eye, row, 0.0), axis=1, keepdims=True)


def neighbours(field):
    lanes = field.shape[1]
    lane = iota(field.shape, 1)
    below = jnp.where(lane == 0, 0.0, pltpu.roll(field, 1, 1))
    above = jnp.where(lane == lanes - 1, 0.0, pltpu.roll(field, lanes - 1, 1))
    return below, field, above


def relu_plus(summed, offset, channels, low=0, high=0, keep_low=None, keep_high=None):
    rows, lanes = summed.shape
    count = rows // channels
    parts = jnp.maximum(summed.reshape(count, channels, lanes) + offset[None], 0.0)
    if low or high:
        pieces = []
        if low:
            pieces.append(parts[:low] * keep_low)
        pieces.append(parts[low : count - high])
        if high:
            pieces.append(parts[count - high :] * keep_high)
        parts = jnp.concatenate([piece for piece in pieces if piece.shape[0]], axis=0)
    return parts.reshape(rows, lanes)


def gather_rows(summed, channels):
    rows, lanes = summed.shape
    taps = summed.reshape(rows // (3 * channels), 3, channels, lanes)
    below, here, above = (taps[:, b].reshape(rows // 3, lanes) for b in range(3))
    lane = iota((rows // 3, 128), 1)
    parts = []
    for n in range(lanes // 128):
        block = slice(128 * n, 128 * n + 128)
        parts.append(
            here[:, block]
            + jnp.where(lane == 0, 0.0, pltpu.roll(below[:, block], 1, 1))
            + jnp.where(lane == 127, 0.0, pltpu.roll(above[:, block], 127, 1))
        )
    return jnp.concatenate(parts, axis=1)


def widen(piece):
    rows, lanes = piece.shape
    return jnp.concatenate([piece.astype(F32), jnp.zeros((rows, 128 - lanes), F32)], axis=1)


def plane_band(weight_ref, band_ref):
    lane = iota((32, 128), 1)
    tiles = [[None] * 5 for _ in range(4)]
    for b in range(3):
        pieces = [widen(weight_ref[3 * a + b]) for a in range(3)]
        base = pieces[0] + pltpu.roll(pieces[1], 32, 1) + pltpu.roll(pieces[2], 64, 1)
        for m in range(4):
            start = 192 * b + 32 * m
            at, off = start // 128, start % 128
            moved = pltpu.roll(base, off, 1) if off else base
            shares = [(at, moved)]
            if off + 96 > 128:
                shares = [(at, jnp.where(lane >= off, moved, 0.0)), (at + 1, jnp.where(lane < off - 32, moved, 0.0))]
            for tile, share in shares:
                old = tiles[m][tile]
                tiles[m][tile] = share if old is None else old + share
    zero = jnp.zeros((32, 128), F32)
    for m in range(4):
        row = [zero if tile is None else tile for tile in tiles[m]]
        band_ref[32 * m : 32 * m + 32, :] = jnp.concatenate(row, axis=1)[:, 0:576].astype(BF16)


def kernel(
    image_hbm, crack_hbm, fold_hbm,
    w1_hbm, b1_hbm, w2_hbm, b2_hbm, wm_hbm, bm_hbm, wd_hbm, bd_hbm, wl_hbm, bl_hbm, wc_hbm, bc_hbm, wh_hbm, bh_hbm,
    out_ref,
    image_ref, crack_ref, fold_ref,
    w1_ref, b1_ref, w2_ref, b2_ref, wm_ref, bm_ref, wd_ref, bd_ref, wl_ref, bl_ref, wc_ref, bc_ref, wh_ref, bh_ref,
    load_sem, swap_send, swap_recv, far_send, far_recv, pass_send, pass_recv,
    half, tile, strip,
    t1, t2, tm, td, tc, tl, th,
    vol, one, two, joined, pooled, mid, deep, lifts, dec,
):
    gz = lax.axis_index("gz")
    xy = lax.axis_index("xy")
    core = lax.rem(xy, 2)
    chip = lax.div(xy, 2)
    last_xy = lax.axis_size("xy") - 1
    keep_low = jnp.where(xy == 0, 0.0, 1.0)
    keep_high = jnp.where(xy == last_xy, 0.0, 1.0)
    twin = (gz, xy + 1 - 2 * core)

    x, y, z = lax.div(chip, 16), lax.rem(lax.div(chip, 4), 4), lax.rem(chip, 4)
    steps = [(i, j, k) for i in range(2) for j in range(4) for k in range(4)]
    steps.sort(key=lambda step: -(2 - abs(2 - step[1]) + 2 - abs(2 - step[2])))
    others = [16 * lax.rem(x + i + 1 - core, 2) + 4 * lax.rem(y + j, 4) + lax.rem(z + k, 4) for i, j, k in steps]

    sources = (
        image_hbm, crack_hbm, fold_hbm,
        w1_hbm, b1_hbm, w2_hbm, b2_hbm, wm_hbm, bm_hbm, wd_hbm, bd_hbm, wl_hbm, bl_hbm, wc_hbm, bc_hbm, wh_hbm, bh_hbm,
    )
    targets = (
        image_ref, crack_ref, fold_ref,
        w1_ref, b1_ref, w2_ref, b2_ref, wm_ref, bm_ref, wd_ref, bd_ref, wl_ref, bl_ref, wc_ref, bc_ref, wh_ref, bh_ref,
    )
    loads = [pltpu.make_async_copy(s, t, load_sem.at[i]) for i, (s, t) in enumerate(zip(sources, targets))]
    for load in loads[:3]:
        load.start()

    barrier = pltpu.get_barrier_semaphore()
    pl.semaphore_signal(barrier, inc=1, device_id=twin, device_id_type=MESH)
    source_gz = jnp.where(core == 1, gz, 1 - gz)
    target_gz = jnp.where(core == 0, gz, 1 - gz)

    for other in others:
        pl.semaphore_signal(barrier, inc=1, device_id=(source_gz, 2 * other + 1 - core), device_id_type=MESH)

    for load in loads[:3]:
        load.wait()
    keep = ((1 - crack_ref[...]) * (1 - fold_ref[...])).astype(F32)
    gated = image_ref[...].astype(F32) * keep
    gated = jnp.concatenate([gated[0], gated[1]], axis=0)
    half[core] = jnp.concatenate([gated[:, :1024], gated[:, 1024:]], axis=0).astype(BF16)

    pl.semaphore_wait(barrier, CHIPS + 1)
    swap = pltpu.make_async_remote_copy(
        src_ref=half.at[core], dst_ref=half.at[core], send_sem=swap_send, recv_sem=swap_recv,
        device_id=twin, device_id_type=MESH,
    )
    swap.start()
    for load in loads[3:]:
        load.start()
    swap.wait()

    sub = iota((8, 128), 0)
    lane = iota((8, 128), 1)
    bands = (half[0].astype(F32), half[1].astype(F32))
    moved = []
    for q in range(2):
        evens, odds = [], []
        for k in range(16):
            rows = slice(8 * (k // 8), 8 * (k // 8) + 8)
            lanes = slice(128 * (k % 8), 128 * (k % 8) + 128)
            low, high = bands[0][rows, lanes], bands[1][rows, lanes]
            if q == 0:
                both = jnp.where(sub < 4, low, pltpu.roll(high, 4, 0))
            else:
                both = jnp.where(sub < 4, pltpu.roll(low, 4, 0), high)
            evens.append(pltpu.roll(both, 16, 1))
            odds.append(pltpu.roll(both, 80, 1))
        moved.append((evens, odds))
    for k in range(16):
        even = [jnp.where(lane >= 16, moved[q][0][k], moved[q][0][max(k - 1, 0)]) for q in range(2)]
        odd = [jnp.where(lane < 80, moved[q][1][k], moved[q][1][min(k + 1, 15)]) for q in range(2)]
        tile[2 * k] = jnp.concatenate(even, axis=0).astype(BF16)
        tile[2 * k + 1] = jnp.concatenate(odd, axis=0).astype(BF16)

    for other in others:
        pltpu.make_async_remote_copy(
            src_ref=tile.at[other], dst_ref=strip.at[0, chip], send_sem=far_send, recv_sem=far_recv,
            device_id=(target_gz, 2 * other + 1 - core), device_id_type=MESH,
        ).start()

    for load in loads[3:]:
        load.wait()
    base = [jnp.zeros((32, 128), F32), jnp.zeros((32, 128), F32)]
    lane = iota((32, 128), 1)
    w1 = w1_ref[...].astype(F32)
    for a in range(3):
        for b in range(3):
            col = column_of(w1[3 * a + b : 3 * a + b + 1])
            base[b // 2] = jnp.where(lane == 64 * (b % 2) + a, col, base[b // 2])
    b1 = column_of(b1_ref[...])
    bias = jnp.zeros((32, 128), F32)
    rest = b1
    for n in range(3):
        part = rest.astype(BF16).astype(F32)
        rest = rest - part
        bias = jnp.where(lane == 64 + n, part, bias)
    for i in range(46):
        pair = (pltpu.roll(base[0], i, 1), pltpu.roll(base[1], i, 1) + bias)
        for n in range(2):
            moved = pair[n] * keep_low if i < 7 else pair[n] * keep_high if i >= 39 else pair[n]
            t1[32 * i : 32 * i + 32, 128 * n : 128 * n + 128] = moved.astype(BF16)
    vol[:, 192:208, :] = jnp.ones((4, 16, 256), BF16)

    plane_band(w2_ref, t2)
    plane_band(wc_ref, tc)

    eye = (iota((64, 64), 0) == iota((64, 64), 1)).astype(BF16)
    for e in range(3):
        place = jnp.where(gz == 0, e, 2 - e)
        for b in range(3):
            rows = [wm_ref[9 * place + 3 * a + b] for a in range(3)]
            base = dot_turned(eye, jnp.concatenate([*rows, jnp.zeros((32, 64), BF16)], axis=0))
            for m in range(2):
                moved = pltpu.roll(base, 32, 1) if m else base
                start = 192 * m + 64 * b
                tm[start : start + 64, 128 * e : 128 * e + 128] = moved.astype(BF16)
            pieces = [widen(wd_ref[9 * place + 3 * a + b]) for a in range(3)]
            turned = [pltpu.roll(piece, 64, 1) for piece in pieces]
            rows = ((pieces[0] + turned[1], pieces[2]), (turned[0], pieces[1] + turned[2]))
            for m in range(2):
                start = 192 * m + 64 * b
                for n in range(2):
                    td[start : start + 64, 256 * e + 128 * n : 256 * e + 128 * n + 128] = rows[m][n].astype(BF16)

    lift = widen(wl_ref[...])
    turned = pltpu.roll(lift, 64, 1)
    blank = jnp.zeros((32, 128), F32)
    for m in range(4):
        piece = turned if m % 2 else lift
        row = [piece, blank] if m < 2 else [blank, piece]
        tl[32 * m : 32 * m + 32, :] = jnp.concatenate(row, axis=1).astype(BF16)
    pick = (iota((32, 256), 0) == lax.rem(iota((32, 256), 1), 32)).astype(BF16)
    wide = dot(wh_ref[...], pick)
    row = iota((24, 256), 0)
    lane = iota((24, 256), 1)
    heads = jnp.zeros((24, 256), F32)
    for k in range(3):
        here = (row // 8 == k) & (row % 8 == lane // 32)
        heads = jnp.where(here, wide[k : k + 1], heads)
    th[...] = heads.astype(BF16)

    b2 = column_of(b2_ref[...])
    bm = column_of(bm_ref[...])
    bd = column_of(bd_ref[...])
    bl = column_of(bl_ref[...])
    bc = column_of(bc_ref[...])
    hrow = iota((24, 1), 0)
    bh_row = bh_ref[...]
    bh = jnp.where(hrow < 8, bh_row[:, 0:1], jnp.where(hrow < 16, bh_row[:, 1:2], bh_row[:, 2:3]))

    pltpu.make_async_copy(strip.at[0], strip.at[0], far_recv).wait()
    hand = pltpu.make_async_remote_copy(
        src_ref=strip.at[0], dst_ref=strip.at[1], send_sem=pass_send, recv_sem=pass_recv,
        device_id=twin, device_id_type=MESH,
    )
    hand.start()

    u = iota((64, 128), 0)
    l = iota((64, 128), 1)
    place = 32 * xy - 8 + u
    inside = (u < 48) & (place >= 0) & (place < 32 * (last_xy + 1))
    select = jnp.where(inside & (l == 8 + 32 * core + u), 1.0, 0.0).astype(BF16)

    fine = iota((256, 128), 0)
    coarse = iota((256, 128), 1)
    pick = jnp.where(fine == 2 * coarse, 1.0, 0.0).astype(BF16)

    def turn(source):
        tiles = strip[source].astype(F32).reshape(CHIPS, 2, 8, 128)
        for q in range(2):
            turned = dot_turned(select, tiles[:, q].reshape(256, 128).astype(BF16))
            for b, part in enumerate(neighbours(turned)):
                vol[2 * source + q, 64 * b : 64 * b + 64, :] = part.astype(BF16)

    def first_layer(p, start, stop):
        rows = slice(32 * start, 32 * stop)
        found = jnp.maximum(dot(t1[rows, 0:208], vol[p]), 0.0)
        for b, part in enumerate(neighbours(found)):
            one[p, b, rows, :] = part.astype(BF16)

    def second_layer(p, g):
        field = jnp.concatenate([one[p, b, 128 * g : 128 * g + 192, :] for b in range(3)], axis=0)
        found = relu_plus(dot(t2[...], field), b2, 32)
        two[p, 128 * g : 128 * g + 128, :] = found.astype(BF16)
        pairs = found.reshape(2, 2, 32, 256)
        pairs = jnp.maximum(pairs[:, 0], pairs[:, 1]).reshape(64, 256)
        pairs = jnp.maximum(pairs, pltpu.roll(pairs, 255, 1))
        joined[p, 64 * g : 64 * g + 64, :] = pairs.astype(BF16)

    def pool(p):
        found = dot(joined[p], pick)
        found = jnp.concatenate([found[:96] * keep_low, found[96:608], found[608:] * keep_high], axis=0).astype(BF16)
        t = jnp.where(core == 1, 2 * (p // 2), 2 - 2 * (p // 2)) + jnp.where(gz == 0, p % 2, 1 - p % 2)
        pooled[:, pl.ds(pl.multiple_of(128 * (t + 1), 128), 128)] = found

    turn(0)
    first_layer(0, 0, 23)
    first_layer(0, 23, 46)
    for p in range(1, 5):
        for g in range(11):
            second_layer(p - 1, g)
            if p == 1 and g == 9:
                hand.wait()
                turn(1)
            if p < 4:
                first_layer(p, 4 * g, 4 * g + 4 if g < 10 else 46)
            if p > 1 and g == 2:
                pool(p - 2)
    pool(3)

    mid[1024:1280, 0:128] = jnp.zeros((256, 128), BF16)
    for g in range(5):
        rows = [slice(128 * g + 64 * h, 128 * g + 64 * h + 128) for h in range(2)]
        field = [jnp.concatenate([pooled[rows[h], 128 * e : 128 * e + 128] for h in range(2)], axis=1) for e in (1, 2)]
        sums = [dot(tm[:, 128:384], jnp.concatenate(field, axis=0))]
        for h in range(2):
            field = [pooled[rows[h], 128 * e + 128 : 128 * e + 384] for e in range(3)]
            sums.append(dot(tm[...], jnp.concatenate(field, axis=0)))
        found = []
        for summed in sums:
            summed = gather_rows(summed, 64)
            found.append(jnp.maximum(summed.reshape(2, 64, 256) + bm[None], 0.0).reshape(128, 256))
        for h in range(2):
            scale = keep_low if g == 0 and h == 0 else keep_high if g == 4 and h == 1 else None
            start = 256 * g + 128 * h
            for part, lanes in ((found[0][:, 128 * h : 128 * h + 128], slice(128, 256)), (found[1 + h], slice(256, 512))):
                if scale is not None:
                    part = part * scale
                mid[start : start + 128, lanes] = part.astype(BF16)

    for g in range(0, 9, 2):
        rows = [slice(128 * i, 128 * i + 256) for i in (g, g + 1)]
        if g < 8:
            sums = []
            for t in range(2):
                field = [
                    jnp.concatenate([mid[row, 128 * (e + t) : 128 * (e + t) + 128] for row in rows], axis=1)
                    for e in range(1 - t, 3)
                ]
                sums.append(dot(td[:, 256 * (1 - t) : 768], jnp.concatenate(field, axis=0)))
        else:
            sums = [dot(td[...], jnp.concatenate([mid[rows[0], 128 * e : 128 * e + 256] for e in range(3)], axis=0))]
        found = []
        for summed in sums:
            summed = gather_rows(summed, 64)
            found.append(jnp.maximum(summed.reshape(2, 64, 256) + bd[None], 0.0).reshape(128, 256).astype(BF16))
        if g < 8:
            for i in range(2):
                start = 128 * (g + i)
                for t in range(2):
                    deep[start : start + 128, 128 * t : 128 * t + 128] = found[t][:, 128 * i : 128 * i + 128]
        else:
            deep[1024:1152, :] = found[0]

    for g in range(5):
        count = 4 if g < 4 else 2
        rows = dot(tl[0 : 32 * count, 0 : 64 * count], deep[256 * g : 256 * g + 64 * count, :])
        rows = (rows.reshape(count, 32, 256) + bl[None]).reshape(32 * count, 256)
        high = rows.astype(BF16)
        low = (rows - high.astype(F32)).astype(BF16)
        for t in range(2):
            both = jnp.concatenate([high[:, 128 * t : 128 * t + 128], low[:, 128 * t : 128 * t + 128]], axis=1)
            lifts[t, 128 * g : 128 * g + 32 * count, :] = both

    fine = iota((256, 256), 1)
    coarse = iota((256, 256), 0)
    double = jnp.where(fine // 2 == coarse % 128, 1.0, 0.0).astype(BF16)
    for g in range(5):
        count = 4 if g < 4 else 2
        for t in range(2):
            lifted = dot(lifts[t, 128 * g : 128 * g + 32 * count, :], double)
            p = jnp.where(core == 1, 0, 2) + jnp.where(gz == 0, t, 1 - t)
            for r in range(count):
                for q in range(2):
                    v = 2 * (4 * g + r) + q
                    old = two[p, 32 * (v + 4) : 32 * (v + 5), :].astype(F32)
                    found = jnp.maximum(lifted[32 * r : 32 * r + 32] + old, 0.0)
                    if v < 2:
                        found = found * keep_low
                    if v >= 34:
                        found = found * keep_high
                    for b, part in enumerate(neighbours(found)):
                        dec[t, b, 32 * v : 32 * v + 32, :] = part.astype(BF16)

    steps = [(g, t) for g in range(4) for t in range(2)]
    fields = []
    for step in range(len(steps) + 8):
        if step < len(steps):
            g, t = steps[step]
            parts = []
            for h in range(2):
                start = g * 256 + 128 * h + 32
                field = jnp.concatenate([dec[t, b, start : start + 192, :] for b in range(3)], axis=0)
                parts.append(relu_plus(dot(tc[...], field), bc, 32).astype(BF16))
            fields.append(jnp.concatenate(parts, axis=0))
        if step >= 8:
            g, t = steps[step - 8]
            found = jax.nn.sigmoid(dot(th[...], fields[step - 8]) + bh)
            s = jnp.where(gz == 0, t, 1 - t)
            for k in range(3):
                out_ref[k, s, 8 * g : 8 * g + 8, :] = found[8 * k : 8 * k + 8]

    pltpu.make_async_copy(tile, tile, far_send).wait()


def body(image, crack, fold, *weights):
    rows = [weight[None] if weight.ndim == 1 else weight for weight in weights]
    rows[4] = jnp.swapaxes(rows[4], 1, 2)
    operands = (image, crack, fold, *rows)
    dma = pltpu.SemaphoreType.DMA
    scratch = [pltpu.VMEM(operand.shape, operand.dtype) for operand in operands]
    scratch += [dma((len(operands),)), dma, dma, dma, dma, dma, dma]
    scratch += [
        pltpu.VMEM(shape, BF16)
        for shape in (
            (2, 16, 1024), (CHIPS, 16, 128), (2, CHIPS, 16, 128),
            (1472, 256), (128, 576), (384, 384), (384, 768), (128, 576), (128, 256), (24, 256),
            (4, 208, 256), (4, 3, 1472, 256), (4, 1408, 256), (4, 704, 256), (704, 640), (1280, 512),
            (1152, 256), (2, 576, 256), (2, 3, 1152, 256),
        )
    ]
    return pl.pallas_call(
        kernel,
        out_shape=pltpu.VMEM((3, 2, 32, 256), F32),
        in_specs=[pl.BlockSpec(memory_space=pl.ANY)] * len(operands),
        out_specs=pl.BlockSpec(memory_space=pltpu.VMEM),
        scratch_shapes=scratch,
        compiler_params=pltpu.CompilerParams(
            collective_id=0, has_side_effects=True, vmem_limit_bytes=60 * 1024 * 1024
        ),
        name="window",
    )(*operands)


def solution(mesh):
    in_specs = (P("gz", "xy", None),) * 3 + (P(),) * 14
    out_specs = P(None, "gz", "xy", None)
    return jax.shard_map(body, mesh=mesh, in_specs=in_specs, out_specs=out_specs, check_vma=False)
```
